512 devices in a mesh: vocab: 8 (over y), row: 8 (over z_hi, core), width: 8 (over z_lo, x).
Axes of the slice: x: 4, y: 8, z: 8 (z_hi: 4, z_lo: 2; z = z_hi * 2 + z_lo), core: 2. Of those that a mesh axis runs over, the one named last changes fastest.
Arguments:
- hidden: bfloat16 [768, 8192], P(None, 'width'), may hold values from -1500 to 1500
- unembed: bfloat16 [8, 4008, 8192], P('vocab', 'row', 'width'), may hold values from -0.06591797 to 0.06591797
- rotate_vocab: bfloat16 [8, 4008, 4008], P('vocab', 'width', 'row'), may hold values from -0.8515625 to 0.8515625
- rotate_width: bfloat16 [8192, 4096], P('width', 'row'), may hold values from -0.0625 to 0.0625
- labels: int32 [768], replicated, may hold values from 0 to 128255
- seq_ids: int32 [768], replicated, may hold values from 0 to 11, never falling along the last dimension, each value on 1 to 128 neighbouring positions
Outputs:
- eigenvalues: float32 [8, 4008, 4096], P('vocab', 'width', 'row')
The draws below stay inside these ranges and needn't reach their ends.
Inputs may be any that keep to these rules, and one draw needn't show every extreme that they name: seq_ids never falls along the tokens; every sequence holds 1 to 128 tokens, one exactly 128.
All inputs are finite; a program needn't handle non-finite values.
Results may differ from the reference program's by a relative error of at most 0.0048.
Values may be sent and summed in bfloat16 or wider, within the bound.
No kernel may reach another device: no remote copies, remote signals or barrier semaphores. Data moves between devices by JAX's collectives and lax.ppermute only.
A program may use at most 64 MiB of HBM per device.

```python
import math
import jax
import jax.numpy as jnp
import numpy as np
from jax import lax

D = 8192
VB = 4008
DJ = 4096
TOK = 768
SEQ_LEN = 128
SEQS = 12
NB = 8
VOCAB = 128256


def draw_hidden(key, part):
    key = jax.random.fold_in(key, 11)
    noise = jnp.clip(jax.random.normal(key, (TOK, D), jnp.float32), -6.0, 6.0)
    common_key = jax.random.fold_in(key, 13)
    common = jnp.clip(jax.random.normal(common_key, (1, D), jnp.float32), -6.0, 6.0)
    base = noise + 1.5 * common
    return base.astype(jnp.bfloat16)


def touch_ends(result, stream_key, low, high):
    spot = [jax.random.randint(jax.random.fold_in(stream_key, axis), (), 0, length) for axis, length in enumerate(result.shape)]
    widest = result.shape.index(max(result.shape))
    next_to = spot[:widest] + [(spot[widest] + 1) % result.shape[widest]] + spot[widest + 1:]
    return result.at[tuple(spot)].set(low).at[tuple(next_to)].set(high)


def block_levels(key, shape, pieces, least, high):
    def one(dim, blocks):
        steps = jax.random.uniform(jax.random.fold_in(jax.random.fold_in(key, 6), dim), (blocks,), jnp.float32, least / len(pieces), high / len(pieces))
        return jnp.repeat(jnp.exp(steps), shape[dim] // blocks).reshape((-1,) + (1,) * (len(shape) - dim - 1))

    gain = one(*pieces[0])
    for cut in pieces[1:]:
        gain = gain * one(*cut)
    return gain


def profile(amount, total, most, skew):
    loads = [(1 << 20) // math.isqrt(standing ** skew) + 1 for standing in range(2, amount + 1)]
    spare, holding = total - most - (amount - 1), [1] * (amount - 1)
    while spare > 0:
        candidates = [i for i in range(amount - 1) if holding[i] < most]
        mass, left = sum([loads[i] for i in candidates]), spare
        for i in candidates:
            addition = min(most - holding[i], max(1, left * loads[i] // mass), spare)
            holding[i] = holding[i] + addition
            spare = spare - addition
    return np.array([most] + holding)


def uneven(own_key, count, total, bound, slope):
    if count == 2:
        one = jax.random.randint(own_key, (), max(1, total - bound), min(bound, total - 1) + 1)
        return jnp.stack([one, total - one])
    lengths = jnp.asarray(profile(count, total, bound, slope), jnp.int32)
    twos = (count - 1) // 2
    giver, taker = lengths[1:1 + 2 * twos:2], lengths[2:2 + 2 * twos:2]
    room = jnp.minimum(giver - 1, bound - taker)
    moved = jax.random.randint(jax.random.fold_in(own_key, 1), (twos,), 0, 1 << 20) % (room + 1)
    lengths = lengths.at[1:1 + 2 * twos:2].set(giver - moved).at[2:2 + 2 * twos:2].set(taker + moved)
    return lengths[jax.random.permutation(jax.random.fold_in(own_key, 2), count)]


def bell_draw(stream_key, extent, deviation, reach, cuts=(), kind=jnp.bfloat16):
    drawn = deviation * jax.random.normal(stream_key, extent, jnp.float32)
    if cuts:
        drawn = drawn * block_levels(stream_key, extent, cuts, -0.22, 0.18)
    return jnp.clip(drawn, -reach, reach).astype(kind)


def setup_inputs(seed: int = 0) -> dict:
    streams_of = jax.random.split(jax.random.key(seed), 7)
    return {
        "hidden": draw_hidden(jax.random.fold_in(streams_of[6], 71), 0),
        "unembed": bell_draw(streams_of[1], (NB, VB, D), (1.0 / D ** 0.5), 0.06591797, ((0, 8), (1, 8), (2, 8))),
        "rotate_vocab": bell_draw(streams_of[2], (NB, VB, VB), (9.0 / VB ** 0.5), 0.8515625, ((0, 8), (1, 8), (2, 8))),
        "rotate_width": bell_draw(streams_of[3], (D, DJ), D ** -0.5, 0.0625, ((0, 8), (1, 8))),
        "labels": touch_ends(jax.random.randint(streams_of[4], (TOK,), 0, VOCAB), jax.random.fold_in(streams_of[4], 1), 0, VOCAB - 1).astype(jnp.int32),
        "seq_ids": jnp.searchsorted(jnp.cumsum(uneven(streams_of[5], SEQS, TOK, SEQ_LEN, 1)), jnp.arange(TOK), side="right").astype(jnp.int32),
    }


def reference(hidden, unembed, rotate_vocab, rotate_width, labels, seq_ids):
    flat = unembed.reshape(NB * VB, D)
    logits = lax.dot_general(hidden, flat, (((1,), (1,)), ((), ())), preferred_element_type=jnp.float32)
    largest = jnp.max(logits, axis=1, keepdims=True)
    scaled = jnp.exp(logits - largest)
    probabilities = scaled / jnp.sum(scaled, axis=1, keepdims=True)
    window_index = jnp.arange(NB * VB, dtype=jnp.int32)
    onehot = (labels[:, None] == window_index[None, :]).astype(jnp.float32)
    errors = (probabilities - onehot).astype(jnp.bfloat16)
    projected = jnp.dot(hidden, rotate_width, preferred_element_type=jnp.float32).astype(jnp.bfloat16)
    error_blocks = errors.reshape(TOK, NB, VB).transpose(1, 0, 2)
    sequence_index = jnp.arange(SEQS, dtype=jnp.int32)
    before = (seq_ids[None, :] < sequence_index[:, None]).astype(jnp.int32)
    starts = jnp.minimum(jnp.sum(before, axis=1), TOK - SEQ_LEN).astype(jnp.int32)

    def one_block(pair):
        eigen_basis, block_errors = pair
        turned = lax.dot_general(block_errors, eigen_basis, (((1,), (1,)), ((), ())), preferred_element_type=jnp.float32).astype(jnp.bfloat16)

        def add_sequence(step, running):
            begin = starts[step].astype(jnp.int32)
            member = lax.dynamic_slice_in_dim(seq_ids, begin, SEQ_LEN, 0) == sequence_index[step]
            turned_rows = lax.dynamic_slice_in_dim(turned, begin, SEQ_LEN, 0)
            masked = jnp.where(member[:, None], turned_rows, jnp.zeros_like(turned_rows))
            projected_rows = lax.dynamic_slice_in_dim(projected, begin, SEQ_LEN, 0)
            gradient = lax.dot_general(masked, projected_rows, (((0,), (0,)), ((), ())), preferred_element_type=jnp.float32)
            return running + gradient * gradient

        return lax.fori_loop(0, SEQS, add_sequence, jnp.zeros((VB, DJ), jnp.float32))

    return lax.map(one_block, (rotate_vocab, error_blocks))
```

```python
import functools

import jax
import jax.numpy as jnp
from jax import lax
from jax.experimental import pallas as pl
from jax.experimental.pallas import tpu as pltpu
from jax.sharding import Mesh
from jax.sharding import PartitionSpec as P

SEQ_LEN = 128
SEQS = 12
PARTS = 8
CORES = 2
CHIPS = PARTS // CORES
TOKENS = 768
GROUP = TOKENS // PARTS
BLOCK = GROUP // CORES
DEALT = BLOCK // PARTS
SHARE = 8
ROWS = BLOCK + SHARE
LANES = 512
WINDOW = SEQ_LEN + 16
VMEM = 48 * 1024 * 1024
MOST = 60 * 1024 * 1024

FULL = pl.BlockSpec(memory_space=pltpu.VMEM)
SCALARS = pl.BlockSpec(memory_space=pltpu.SMEM)
ROW = ("chip", "core")


def call(kernel, outs, ins):
    shapes = [jax.ShapeDtypeStruct(s, d) for s, d in outs]
    return pl.pallas_call(
        kernel,
        out_shape=shapes if len(shapes) > 1 else shapes[0],
        in_specs=ins,
        out_specs=[FULL] * len(shapes) if len(shapes) > 1 else FULL,
        compiler_params=pltpu.CompilerParams(vmem_limit_bytes=VMEM),
    )


def pick(shape, source):
    row = lax.broadcasted_iota(jnp.int32, shape, 0)
    column = lax.broadcasted_iota(jnp.int32, shape, 1)
    return (column == source(row)).astype(jnp.float32).astype(jnp.bfloat16)


def partial_kernel(place_ref, hidden_ref, mine_ref, unembed_ref, width_ref, out_ref):
    rows = unembed_ref.shape[1]
    cores, each = out_ref.shape[:2]
    logits = lax.dot_general(
        hidden_ref[...], unembed_ref[0], (((1,), (1,)), ((), ())), preferred_element_type=jnp.float32
    )
    first = pl.program_id(0) * each

    def source(row):
        piece, within = row // SHARE, lax.rem(row, SHARE)
        owner = (first + lax.rem(piece, each)) * cores + piece // each
        return jnp.where(within < DEALT, owner * DEALT + within, -1)

    dealt = jnp.dot(pick((cores * each * SHARE, GROUP), source), mine_ref[...], preferred_element_type=jnp.float32)
    projected = jnp.dot(dealt.astype(jnp.bfloat16), width_ref[...], preferred_element_type=jnp.float32)
    for core in range(cores):
        for width in range(each):
            piece = core * each + width
            out_ref[core, width, :BLOCK, rows:] = jnp.zeros((BLOCK, LANES - rows), jnp.float32)
            out_ref[core, width, :BLOCK, :rows] = logits[piece * BLOCK : (piece + 1) * BLOCK]
            out_ref[core, width, BLOCK:, :] = projected[piece * SHARE : (piece + 1) * SHARE]


def partial_sums(place, hidden, unembed, rotate_width):
    each = PARTS // CHIPS
    features, columns = rotate_width.shape
    rows = unembed.shape[1]
    return pl.pallas_call(
        partial_kernel,
        out_shape=jax.ShapeDtypeStruct((CORES, PARTS, ROWS, LANES), jnp.float32),
        grid_spec=pltpu.PrefetchScalarGridSpec(
            num_scalar_prefetch=1,
            grid=(CHIPS,),
            in_specs=[
                pl.BlockSpec((CORES * GROUP, features), lambda g, place: (g, 0)),
                pl.BlockSpec((GROUP, features), lambda g, place: (place[0], 0)),
                pl.BlockSpec((1, rows, features), lambda g, place: (0, 0, 0)),
                pl.BlockSpec((features, columns), lambda g, place: (0, 0)),
            ],
            out_specs=pl.BlockSpec((CORES, each, ROWS, LANES), lambda g, place: (0, g, 0, 0)),
        ),
        compiler_params=pltpu.CompilerParams(vmem_limit_bytes=MOST),
    )(place, hidden, hidden, unembed, rotate_width)


def local_kernel(rows, core_ref, pieces_ref, logits_ref, stats_ref, keep_ref, send_ref):
    sums = [jnp.sum(pieces_ref[core * PARTS : (core + 1) * PARTS], axis=0) for core in range(CORES)]
    column = lax.broadcasted_iota(jnp.int32, (CORES * BLOCK, LANES), 1)
    logits = jnp.concatenate([part[:BLOCK] for part in sums], axis=0)
    logits = jnp.where(column < rows, logits, -jnp.inf)
    logits_ref[...] = logits
    first = core_ref[0] == 0
    keep_ref[...] = jnp.where(first, sums[0][BLOCK:], sums[1][BLOCK:])
    send_ref[...] = jnp.where(first, sums[1][BLOCK:], sums[0][BLOCK:])
    largest = jnp.max(logits, axis=1, keepdims=True)
    largest = jnp.maximum(largest[:BLOCK], largest[BLOCK:])
    total = jnp.sum(jnp.exp(logits - jnp.concatenate([largest, largest], axis=0)), axis=1, keepdims=True)
    total = total[:BLOCK] + total[BLOCK:]
    lane = lax.broadcasted_iota(jnp.int32, (BLOCK, 128), 1)
    square = jnp.concatenate(
        [jnp.where(lane == 0, largest, total), jnp.zeros((128 - BLOCK, 128), jnp.float32)], axis=0
    )
    tile = square.T[: stats_ref.shape[1]]
    for device in range(stats_ref.shape[0]):
        stats_ref[device] = tile


def error_kernel(rows, place_ref, logits_ref, stats_ref, labels_ref, keep_ref, got_ref, out_ref):
    largest = jnp.max(stats_ref[:, 0:1, :], axis=0)
    total = jnp.sum(stats_ref[:, 1:2, :] * jnp.exp(stats_ref[:, 0:1, :] - largest[None]), axis=0)
    row = lax.broadcasted_iota(jnp.int32, (128, 128), 0)
    square = jnp.where(row == 0, largest, total).T
    largest, total = square[:BLOCK, 0:1], square[:BLOCK, 1:2]
    column = lax.broadcasted_iota(jnp.int32, (BLOCK, LANES), 1)
    parts = []
    for core in range(CORES):
        probabilities = jnp.exp(logits_ref[core * BLOCK : (core + 1) * BLOCK] - largest) / total
        hit = (labels_ref[...] - (place_ref[1] + core * rows) == column) & (column < rows)
        parts.append((probabilities - hit.astype(jnp.float32)).astype(jnp.bfloat16))
    errors = jnp.concatenate(parts, axis=0)
    first = place_ref[0] == 0
    keep, got = keep_ref[...], got_ref[...]
    share = jnp.concatenate([jnp.where(first, keep, got), jnp.where(first, got, keep)], axis=0).astype(jnp.bfloat16)
    for piece in range(PARTS):
        out_ref[piece, : CORES * BLOCK] = errors
        out_ref[piece, CORES * BLOCK :] = share


def turn_kernel(core_ref, packed_ref, basis_ref, other_ref, out_ref, share_ref):
    rows = basis_ref.shape[1]
    turned = 0.0
    for core, ref in ((core_ref[0], basis_ref), (1 - core_ref[0], other_ref)):
        errors = packed_ref[:, pl.ds(pl.multiple_of(core * BLOCK, BLOCK), BLOCK), :].reshape(PARTS * BLOCK, LANES)
        turned += lax.dot_general(
            errors[:, :rows], ref[0], (((1,), (1,)), ((), ())), preferred_element_type=jnp.float32
        )
    out_ref[:, :, :rows] = turned.astype(jnp.bfloat16).reshape(CHIPS, GROUP, rows)
    out_ref[:, :, rows:] = jnp.zeros((CHIPS, GROUP, LANES - rows), jnp.bfloat16)
    dealt = packed_ref[:, CORES * BLOCK :, :].reshape(PARTS * CORES * SHARE, LANES)
    order = pick((GROUP, PARTS * CORES * SHARE), lambda row: row // DEALT * SHARE + lax.rem(row, DEALT))
    share = jnp.dot(order, dealt, preferred_element_type=jnp.float32).astype(jnp.bfloat16)
    for piece in range(PARTS):
        share_ref[piece] = share


def sum_kernel(pieces_ref, out_ref):
    out_ref[...] = jnp.sum(pieces_ref[...].astype(jnp.float32), axis=0).astype(jnp.bfloat16)


def gradient_kernel(starts_ref, turned_ref, projected_ref, out_ref, total_ref):
    for sequence in range(SEQS):
        start, end = starts_ref[sequence], starts_ref[sequence + 1]
        begin = pl.multiple_of(jnp.minimum(start // 16 * 16, TOKENS - WINDOW), 16)
        token = begin + lax.broadcasted_iota(jnp.int32, (WINDOW, 1), 0)
        member = (token >= start) & (token < end)
        turned = turned_ref[pl.ds(begin, WINDOW), :]
        turned = jnp.where(member, turned, jnp.zeros((), jnp.bfloat16))
        gradient = lax.dot_general(
            turned,
            projected_ref[pl.ds(begin, WINDOW), :],
            (((0,), (0,)), ((), ())),
            preferred_element_type=jnp.float32,
        )
        if sequence == 0:
            total_ref[...] = gradient * gradient
        elif sequence < SEQS - 1:
            total_ref[...] += gradient * gradient
        else:
            total = total_ref[...] + gradient * gradient
            tile, width = total.shape
            pieces = width // 128
            for piece in range(pieces):
                out_ref[pl.ds(piece, tile, stride=pieces), :] = total[:, piece * 128 : (piece + 1) * 128]


def gradients(starts, turned, projected, height):
    width = projected.shape[1]
    tile, pieces = 128, width // 128
    flat = pl.pallas_call(
        gradient_kernel,
        out_shape=jax.ShapeDtypeStruct((height * pieces, 128), jnp.float32),
        grid_spec=pltpu.PrefetchScalarGridSpec(
            num_scalar_prefetch=1,
            grid=(LANES // tile,),
            in_specs=[
                pl.BlockSpec((TOKENS, tile), lambda g, starts: (0, g)),
                pl.BlockSpec((TOKENS, width), lambda g, starts: (0, 0)),
            ],
            out_specs=pl.BlockSpec((tile * pieces, 128), lambda g, starts: (g, 0)),
            scratch_shapes=[pltpu.VMEM((tile, width), jnp.float32)],
        ),
        compiler_params=pltpu.CompilerParams(vmem_limit_bytes=VMEM),
    )(starts, turned, projected)
    return flat.reshape(1, height, width)


def exchange(values, axis):
    return lax.all_to_all(values, axis, 0, 0, tiled=True)


def swap(values):
    return lax.ppermute(values, "core", [(i, CORES - 1 - i) for i in range(CORES)])


def body(hidden, unembed, rotate_vocab, rotate_width, labels, seq_ids):
    rows = unembed.shape[1]
    vocab, chip, core, width = (lax.axis_index(a).astype(jnp.int32) for a in ("vocab", "chip", "core", "width"))
    place = jnp.stack([core, (vocab * PARTS + chip * CORES) * rows])
    core = core.reshape(1)
    owned = (width // CORES * CORES + core[0]) * GROUP + lax.rem(width, CORES) * BLOCK
    mine = lax.dynamic_slice_in_dim(labels, owned, BLOCK, 0).reshape(BLOCK, 1)
    sequence_index = jnp.arange(SEQS + 1, dtype=jnp.int32)
    starts = jnp.sum((seq_ids[None, :] < sequence_index[:, None]).astype(jnp.int32), axis=1)
    half, single = jnp.bfloat16, jnp.float32

    pieces = partial_sums(vocab.reshape(1), hidden, unembed, rotate_width)
    pieces = exchange(pieces.reshape(CORES * PARTS, ROWS, LANES), ("core", "width"))
    logits, stats, keep, send = call(
        functools.partial(local_kernel, rows),
        [
            ((CORES * BLOCK, LANES), single),
            ((PARTS * CHIPS, 2, 128), single),
            ((SHARE, LANES), single),
            ((SHARE, LANES), single),
        ],
        [SCALARS, FULL],
    )(core, pieces)
    stats = exchange(stats, ("vocab", "chip"))
    packed = call(
        functools.partial(error_kernel, rows),
        [((PARTS, CORES * ROWS, LANES), half)],
        [SCALARS, FULL, FULL, FULL, FULL, FULL],
    )(place, logits, stats, mine, keep, swap(send))
    turned, share = call(
        turn_kernel,
        [((CHIPS, GROUP, LANES), half), ((PARTS, GROUP, LANES), half)],
        [SCALARS, FULL, FULL, FULL],
    )(core, exchange(packed, "width"), rotate_vocab, swap(rotate_vocab))
    projected = exchange(share, "vocab").reshape(TOKENS, LANES)
    turned = call(sum_kernel, [((GROUP, LANES), half)], [FULL])(exchange(turned, "chip"))
    turned = lax.all_gather(turned, ROW, axis=0, tiled=True)
    return gradients(starts, turned, projected, rows)


def solution(mesh):
    vocab, row, width = mesh.axis_names
    devices = mesh.devices.reshape(PARTS, CHIPS, CORES, PARTS)
    in_specs = (
        P(None, width),
        P(vocab, ROW, width),
        P(vocab, width, ROW),
        P(width, ROW),
        P(),
        P(),
    )
    return jax.shard_map(
        body,
        mesh=Mesh(devices, (vocab, *ROW, width)),
        in_specs=in_specs,
        out_specs=P(vocab, width, ROW),
        check_vma=False,
    )
```

```python
import functools

import jax
import jax.numpy as jnp
from jax import lax
from jax.experimental import pallas as pl
from jax.experimental.pallas import tpu as pltpu
from jax.sharding import Mesh
from jax.sharding import PartitionSpec as P

SEQ_LEN = 128
SEQS = 12
PARTS = 8
CORES = 2
CHIPS = PARTS // CORES
TOKENS = 768
GROUP = TOKENS // PARTS
BLOCK = GROUP // CORES
DEALT = BLOCK // PARTS
SHARE = 8
ROWS = BLOCK + SHARE
LANES = 512
WINDOW = SEQ_LEN + 16
VMEM = 48 * 1024 * 1024
MOST = 60 * 1024 * 1024

FULL = pl.BlockSpec(memory_space=pltpu.VMEM)
SCALARS = pl.BlockSpec(memory_space=pltpu.SMEM)
ROW = ("chip", "core")


def call(kernel, outs, ins):
    shapes = [jax.ShapeDtypeStruct(s, d) for s, d in outs]
    return pl.pallas_call(
        kernel,
        out_shape=shapes if len(shapes) > 1 else shapes[0],
        in_specs=ins,
        out_specs=[FULL] * len(shapes) if len(shapes) > 1 else FULL,
        compiler_params=pltpu.CompilerParams(vmem_limit_bytes=VMEM),
    )


def pick(shape, source):
    row = lax.broadcasted_iota(jnp.int32, shape, 0)
    column = lax.broadcasted_iota(jnp.int32, shape, 1)
    return (column == source(row)).astype(jnp.float32).astype(jnp.bfloat16)


def owned(core, width):
    return (width // CORES * CORES + core) * GROUP + width % CORES * BLOCK


def partial_kernel(place_ref, hidden_ref, mine_ref, unembed_ref, width_ref, out_ref):
    rows = unembed_ref.shape[1]
    logits = lax.dot_general(
        hidden_ref[...], unembed_ref[0], (((1,), (1,)), ((), ())), preferred_element_type=jnp.float32
    )

    def source(row):
        core, width, within = row // (PARTS * SHARE), lax.rem(row // SHARE, PARTS), lax.rem(row, SHARE)
        return jnp.where(within < DEALT, (width * CORES + core) * DEALT + within, -1)

    dealt = jnp.dot(pick((CORES * PARTS * SHARE, GROUP), source), mine_ref[...], preferred_element_type=jnp.float32)
    projected = jnp.dot(dealt.astype(jnp.bfloat16), width_ref[...], preferred_element_type=jnp.float32)
    for core in range(CORES):
        for width in range(PARTS):
            owner, begin = core * PARTS + width, owned(core, width)
            out_ref[owner, :BLOCK, rows:] = jnp.zeros((BLOCK, LANES - rows), jnp.float32)
            out_ref[owner, :BLOCK, :rows] = logits[begin : begin + BLOCK]
            out_ref[owner, BLOCK:, :] = projected[owner * SHARE : (owner + 1) * SHARE]


def partial_sums(place, hidden, unembed, rotate_width):
    return pl.pallas_call(
        partial_kernel,
        out_shape=jax.ShapeDtypeStruct((CORES * PARTS, ROWS, LANES), jnp.float32),
        grid_spec=pltpu.PrefetchScalarGridSpec(
            num_scalar_prefetch=1,
            grid=(1,),
            in_specs=[
                pl.BlockSpec(hidden.shape, lambda g, place: (0, 0)),
                pl.BlockSpec((GROUP, hidden.shape[1]), lambda g, place: (place[0], 0)),
                pl.BlockSpec(unembed.shape, lambda g, place: (0, 0, 0)),
                pl.BlockSpec(rotate_width.shape, lambda g, place: (0, 0)),
            ],
            out_specs=pl.BlockSpec((CORES * PARTS, ROWS, LANES), lambda g, place: (0, 0, 0)),
        ),
        compiler_params=pltpu.CompilerParams(vmem_limit_bytes=MOST),
    )(place, hidden, hidden, unembed, rotate_width)


def local_kernel(rows, core_ref, pieces_ref, logits_ref, stats_ref, keep_ref, send_ref):
    sums = [jnp.sum(pieces_ref[core * PARTS : (core + 1) * PARTS], axis=0) for core in range(CORES)]
    column = lax.broadcasted_iota(jnp.int32, (CORES * BLOCK, LANES), 1)
    logits = jnp.concatenate([part[:BLOCK] for part in sums], axis=0)
    logits = jnp.where(column < rows, logits, -jnp.inf)
    logits_ref[...] = logits
    first = core_ref[0] == 0
    keep_ref[...] = jnp.where(first, sums[0][BLOCK:], sums[1][BLOCK:])
    send_ref[...] = jnp.where(first, sums[1][BLOCK:], sums[0][BLOCK:])
    largest = jnp.max(logits, axis=1, keepdims=True)
    largest = jnp.maximum(largest[:BLOCK], largest[BLOCK:])
    total = jnp.sum(jnp.exp(logits - jnp.concatenate([largest, largest], axis=0)), axis=1, keepdims=True)
    total = total[:BLOCK] + total[BLOCK:]
    lane = lax.broadcasted_iota(jnp.int32, (BLOCK, 128), 1)
    square = jnp.concatenate(
        [jnp.where(lane == 0, largest, total), jnp.zeros((128 - BLOCK, 128), jnp.float32)], axis=0
    )
    tile = square.T[: stats_ref.shape[1]]
    for device in range(stats_ref.shape[0]):
        stats_ref[device] = tile


def error_kernel(rows, place_ref, logits_ref, stats_ref, labels_ref, keep_ref, got_ref, out_ref):
    largest = jnp.max(stats_ref[:, 0:1, :], axis=0)
    total = jnp.sum(stats_ref[:, 1:2, :] * jnp.exp(stats_ref[:, 0:1, :] - largest[None]), axis=0)
    row = lax.broadcasted_iota(jnp.int32, (128, 128), 0)
    square = jnp.where(row == 0, largest, total).T
    largest, total = square[:BLOCK, 0:1], square[:BLOCK, 1:2]
    column = lax.broadcasted_iota(jnp.int32, (BLOCK, LANES), 1)
    parts = []
    for core in range(CORES):
        probabilities = jnp.exp(logits_ref[core * BLOCK : (core + 1) * BLOCK] - largest) / total
        hit = (labels_ref[...] - (place_ref[1] + core * rows) == column) & (column < rows)
        parts.append((probabilities - hit.astype(jnp.float32)).astype(jnp.bfloat16))
    errors = jnp.concatenate(parts, axis=0)
    first = place_ref[0] == 0
    keep, got = keep_ref[...], got_ref[...]
    share = jnp.concatenate([jnp.where(first, keep, got), jnp.where(first, got, keep)], axis=0).astype(jnp.bfloat16)
    for piece in range(PARTS):
        out_ref[piece, : CORES * BLOCK] = errors
        out_ref[piece, CORES * BLOCK :] = share


def turn_kernel(core_ref, packed_ref, basis_ref, other_ref, starts_ref, out_ref, share_ref):
    rows = basis_ref.shape[1]
    turned = 0.0
    for core, ref in ((core_ref[0], basis_ref), (1 - core_ref[0], other_ref)):
        errors = packed_ref[:, pl.ds(pl.multiple_of(core * BLOCK, BLOCK), BLOCK), :].reshape(PARTS * BLOCK, LANES)
        turned += lax.dot_general(
            errors[:, :rows], ref[0], (((1,), (1,)), ((), ())), preferred_element_type=jnp.float32
        )
    out_ref[:, :, :rows] = turned.astype(jnp.bfloat16).reshape(CHIPS, GROUP, rows)
    out_ref[:, :, rows:] = jnp.zeros((CHIPS, GROUP, LANES - rows), jnp.bfloat16)
    dealt = packed_ref[:, CORES * BLOCK :, :].reshape(PARTS * CORES * SHARE, LANES)
    order = pick((GROUP, PARTS * CORES * SHARE), lambda row: row // DEALT * SHARE + lax.rem(row, DEALT))
    share = jnp.dot(order, dealt, preferred_element_type=jnp.float32).astype(jnp.bfloat16)
    for piece in range(PARTS):
        share_ref[piece] = share


def sum_kernel(pieces_ref, out_ref):
    out_ref[...] = jnp.sum(pieces_ref[...].astype(jnp.float32), axis=0).astype(jnp.bfloat16)


def gradient_kernel(starts_ref, turned_ref, projected_ref, out_ref, total_ref):
    for sequence in range(SEQS):
        start, end = starts_ref[sequence], starts_ref[sequence + 1]
        begin = pl.multiple_of(jnp.minimum(start // 16 * 16, TOKENS - WINDOW), 16)
        token = begin + lax.broadcasted_iota(jnp.int32, (WINDOW, 1), 0)
        member = (token >= start) & (token < end)
        turned = turned_ref[pl.ds(begin, WINDOW), :]
        turned = jnp.where(member, turned, jnp.zeros((), jnp.bfloat16))
        gradient = lax.dot_general(
            turned,
            projected_ref[pl.ds(begin, WINDOW), :],
            (((0,), (0,)), ((), ())),
            preferred_element_type=jnp.float32,
        )
        if sequence == 0:
            total_ref[...] = gradient * gradient
        elif sequence < SEQS - 1:
            total_ref[...] += gradient * gradient
        else:
            out_ref[...] = (total_ref[...] + gradient * gradient).reshape(out_ref.shape)


def gradients(starts, turned, projected, height):
    width = projected.shape[1]
    tile = 256
    out = pl.pallas_call(
        gradient_kernel,
        out_shape=jax.ShapeDtypeStruct((height, 1, width), jnp.float32),
        grid_spec=pltpu.PrefetchScalarGridSpec(
            num_scalar_prefetch=1,
            grid=(LANES // tile,),
            in_specs=[
                pl.BlockSpec((TOKENS, tile), lambda g, starts: (0, g)),
                pl.BlockSpec((TOKENS, width), lambda g, starts: (0, 0)),
            ],
            out_specs=pl.BlockSpec((tile, 1, width), lambda g, starts: (g, 0, 0)),
            scratch_shapes=[pltpu.VMEM((tile, width), jnp.float32)],
        ),
        compiler_params=pltpu.CompilerParams(vmem_limit_bytes=16 * 1024 * 1024),
    )(starts, turned, projected)
    return out.transpose(1, 0, 2)


def exchange(values, axis):
    return lax.all_to_all(values, axis, 0, 0, tiled=True)


def swap(values):
    return lax.ppermute(values, "core", [(i, CORES - 1 - i) for i in range(CORES)])


def body(hidden, unembed, rotate_vocab, rotate_width, labels, seq_ids):
    rows = unembed.shape[1]
    vocab, chip, core, width = (lax.axis_index(a).astype(jnp.int32) for a in ("vocab", "chip", "core", "width"))
    place = jnp.stack([core, (vocab * PARTS + chip * CORES) * rows])
    core = core.reshape(1)
    mine = lax.dynamic_slice_in_dim(labels, owned(core[0], width), BLOCK, 0).reshape(BLOCK, 1)
    sequence_index = jnp.arange(SEQS + 1, dtype=jnp.int32)
    starts = jnp.sum((seq_ids[None, :] < sequence_index[:, None]).astype(jnp.int32), axis=1)
    half, single = jnp.bfloat16, jnp.float32

    pieces = partial_sums(vocab.reshape(1), hidden, unembed, rotate_width)
    pieces = exchange(pieces, ("core", "width"))
    logits, stats, keep, send = call(
        functools.partial(local_kernel, rows),
        [
            ((CORES * BLOCK, LANES), single),
            ((PARTS * CHIPS, 2, 128), single),
            ((SHARE, LANES), single),
            ((SHARE, LANES), single),
        ],
        [SCALARS, FULL],
    )(core, pieces)
    stats = exchange(stats, ("vocab", "chip"))
    packed = call(
        functools.partial(error_kernel, rows),
        [((PARTS, CORES * ROWS, LANES), half)],
        [SCALARS, FULL, FULL, FULL, FULL, FULL],
    )(place, logits, stats, mine, keep, swap(send))
    turned, share = call(
        turn_kernel,
        [((CHIPS, GROUP, LANES), half), ((PARTS, GROUP, LANES), half)],
        [SCALARS, FULL, FULL, FULL, pl.BlockSpec(memory_space=pl.ANY)],
    )(core, exchange(packed, "width"), rotate_vocab, swap(rotate_vocab), starts)
    projected = exchange(share, "vocab").reshape(TOKENS, LANES)
    turned = call(sum_kernel, [((GROUP, LANES), half)], [FULL])(exchange(turned, "chip"))
    turned = lax.all_gather(turned, ROW, axis=0, tiled=True)
    return gradients(starts, turned, projected, rows)


def solution(mesh):
    vocab, row, width = mesh.axis_names
    devices = mesh.devices.reshape(PARTS, CHIPS, CORES, PARTS)
    in_specs = (
        P(None, width),
        P(vocab, ROW, width),
        P(vocab, width, ROW),
        P(width, ROW),
        P(),
        P(),
    )
    return jax.shard_map(
        body,
        mesh=Mesh(devices, (vocab, *ROW, width)),
        in_specs=in_specs,
        out_specs=P(vocab, width, ROW),
        check_vma=False,
    )
```

```python
import functools

import jax
import jax.numpy as jnp
from jax import lax
from jax.experimental import pallas as pl
from jax.experimental.pallas import tpu as pltpu
from jax.sharding import Mesh
from jax.sharding import PartitionSpec as P

SEQ_LEN = 128
SEQS = 12
PARTS = 8
CORES = 2
CHIPS = PARTS // CORES
TOKENS = 768
GROUP = TOKENS // PARTS
BLOCK = GROUP // CORES
DEALT = BLOCK // PARTS
SHARE = 8
ROWS = BLOCK + SHARE
SENT = 16
LANES = 512
WINDOW = SEQ_LEN + 16
VMEM = 48 * 1024 * 1024
MOST = 60 * 1024 * 1024

FULL = pl.BlockSpec(memory_space=pltpu.VMEM)
SCALARS = pl.BlockSpec(memory_space=pltpu.SMEM)
ROW = ("chip", "core")


def call(kernel, outs, ins):
    shapes = [jax.ShapeDtypeStruct(s, d) for s, d in outs]
    return pl.pallas_call(
        kernel,
        out_shape=shapes if len(shapes) > 1 else shapes[0],
        in_specs=ins,
        out_specs=[FULL] * len(shapes) if len(shapes) > 1 else FULL,
        compiler_params=pltpu.CompilerParams(vmem_limit_bytes=VMEM),
    )


def pick(shape, source):
    row = lax.broadcasted_iota(jnp.int32, shape, 0)
    column = lax.broadcasted_iota(jnp.int32, shape, 1)
    return (column == source(row)).astype(jnp.float32).astype(jnp.bfloat16)


def owned(core, width):
    return (width // CORES * CORES + core) * GROUP + width % CORES * BLOCK


def step_of(exponent):
    return jnp.exp2(exponent)


def encode(values):
    top, low = jnp.max(values, axis=1, keepdims=True), jnp.min(values, axis=1, keepdims=True)
    middle, radius = 0.5 * top + 0.5 * low, 0.5 * top - 0.5 * low
    least = jnp.maximum(jnp.maximum(radius / 32000.0, jnp.abs(middle) * 2.0**-29), 2.0**-100)
    exponent = jnp.ceil(jnp.log2(least))
    step = step_of(exponent)
    offset = jnp.floor(middle / step + 0.5)
    return jnp.floor((values - offset * step) / step + 0.5), exponent, offset


def whole(values):
    return values.astype(jnp.int32).astype(jnp.int16)


def partial_kernel(place_ref, hidden_ref, mine_ref, unembed_ref, width_ref, out_ref):
    rows = unembed_ref.shape[1]
    logits = lax.dot_general(
        hidden_ref[...], unembed_ref[0], (((1,), (1,)), ((), ())), preferred_element_type=jnp.float32
    )

    def source(row):
        core, width, within = row // (PARTS * SENT), lax.rem(row // SENT, PARTS), lax.rem(row, SENT)
        return jnp.where(within < DEALT, (width * CORES + core) * DEALT + within, -1)

    dealt = jnp.dot(pick((CORES * PARTS * SENT, GROUP), source), mine_ref[...], preferred_element_type=jnp.float32)
    projected = jnp.dot(dealt.astype(jnp.bfloat16), width_ref[...], preferred_element_type=jnp.float32)
    projected, share_exponent, share_offset = encode(projected)
    logits, exponent, offset = encode(logits)
    high = jnp.floor(offset / 32768.0)
    share_high = jnp.floor(share_offset / 32768.0)
    lane = lax.broadcasted_iota(jnp.int32, (BLOCK, LANES - rows), 1)
    for core in range(CORES):
        for width in range(PARTS):
            owner, begin = core * PARTS + width, owned(core, width)
            tokens, shares = slice(begin, begin + BLOCK), slice(owner * SENT, (owner + 1) * SENT)
            notes = jnp.where(lane == 0, exponent[tokens], 0.0)
            notes = jnp.where(lane == 1, high[tokens], notes)
            notes = jnp.where(lane == 2, offset[tokens] - high[tokens] * 32768.0, notes)
            rest = jnp.zeros((BLOCK - SENT, 1), jnp.float32)
            for number, part in enumerate(
                (share_exponent[shares], share_high[shares], share_offset[shares] - share_high[shares] * 32768.0)
            ):
                notes = jnp.where(lane == 3 + number, jnp.concatenate([part, rest], axis=0), notes)
            out_ref[owner, :BLOCK, :rows] = whole(logits[tokens])
            out_ref[owner, :BLOCK, rows:] = whole(notes)
            out_ref[owner, BLOCK:, :] = whole(projected[shares])


def partial_sums(place, hidden, unembed, rotate_width):
    return pl.pallas_call(
        partial_kernel,
        out_shape=jax.ShapeDtypeStruct((CORES * PARTS, BLOCK + SENT, LANES), jnp.int16),
        grid_spec=pltpu.PrefetchScalarGridSpec(
            num_scalar_prefetch=1,
            grid=(1,),
            in_specs=[
                pl.BlockSpec(hidden.shape, lambda g, place: (0, 0)),
                pl.BlockSpec((GROUP, hidden.shape[1]), lambda g, place: (place[0], 0)),
                pl.BlockSpec(unembed.shape, lambda g, place: (0, 0, 0)),
                pl.BlockSpec(rotate_width.shape, lambda g, place: (0, 0)),
            ],
            out_specs=pl.BlockSpec((CORES * PARTS, BLOCK + SENT, LANES), lambda g, place: (0, 0, 0)),
        ),
        compiler_params=pltpu.CompilerParams(vmem_limit_bytes=MOST),
    )(place, hidden, hidden, unembed, rotate_width)


def decode(rows, pieces_ref, owner):
    values = pieces_ref[owner].astype(jnp.int32).astype(jnp.float32)
    notes = values[:BLOCK, rows:]
    step = step_of(notes[:, 0:1])
    logits = values[:BLOCK] * step + (notes[:, 1:2] * 32768.0 + notes[:, 2:3]) * step
    notes = notes[:SHARE]
    step = step_of(notes[:, 3:4])
    share = values[BLOCK : BLOCK + SHARE] * step + (notes[:, 4:5] * 32768.0 + notes[:, 5:6]) * step
    return jnp.concatenate([logits, share], axis=0)


def local_kernel(rows, core_ref, pieces_ref, logits_ref, stats_ref, keep_ref, send_ref):
    sums = [sum(decode(rows, pieces_ref, core * PARTS + width) for width in range(PARTS)) for core in range(CORES)]
    column = lax.broadcasted_iota(jnp.int32, (CORES * BLOCK, LANES), 1)
    logits = jnp.concatenate([part[:BLOCK] for part in sums], axis=0)
    logits = jnp.where(column < rows, logits, -jnp.inf)
    logits_ref[...] = logits
    first = core_ref[0] == 0
    keep_ref[...] = jnp.where(first, sums[0][BLOCK:], sums[1][BLOCK:])
    send_ref[...] = jnp.where(first, sums[1][BLOCK:], sums[0][BLOCK:])
    largest = jnp.max(logits, axis=1, keepdims=True)
    largest = jnp.maximum(largest[:BLOCK], largest[BLOCK:])
    total = jnp.sum(jnp.exp(logits - jnp.concatenate([largest, largest], axis=0)), axis=1, keepdims=True)
    total = total[:BLOCK] + total[BLOCK:]
    lane = lax.broadcasted_iota(jnp.int32, (BLOCK, 128), 1)
    square = jnp.concatenate(
        [jnp.where(lane == 0, largest, total), jnp.zeros((128 - BLOCK, 128), jnp.float32)], axis=0
    )
    tile = square.T[: stats_ref.shape[1]]
    for device in range(stats_ref.shape[0]):
        stats_ref[device] = tile


def error_kernel(rows, place_ref, logits_ref, stats_ref, labels_ref, keep_ref, got_ref, out_ref):
    largest = jnp.max(stats_ref[:, 0:1, :], axis=0)
    total = jnp.sum(stats_ref[:, 1:2, :] * jnp.exp(stats_ref[:, 0:1, :] - largest[None]), axis=0)
    row = lax.broadcasted_iota(jnp.int32, (128, 128), 0)
    square = jnp.where(row == 0, largest, total).T
    largest, total = square[:BLOCK, 0:1], square[:BLOCK, 1:2]
    column = lax.broadcasted_iota(jnp.int32, (BLOCK, LANES), 1)
    parts = []
    for core in range(CORES):
        probabilities = jnp.exp(logits_ref[core * BLOCK : (core + 1) * BLOCK] - largest) / total
        hit = (labels_ref[...] - (place_ref[1] + core * rows) == column) & (column < rows)
        parts.append((probabilities - hit.astype(jnp.float32)).astype(jnp.bfloat16))
    errors = jnp.concatenate(parts, axis=0)
    first = place_ref[0] == 0
    keep, got = keep_ref[...], got_ref[...]
    share = jnp.concatenate([jnp.where(first, keep, got), jnp.where(first, got, keep)], axis=0).astype(jnp.bfloat16)
    for piece in range(PARTS):
        out_ref[piece, : CORES * BLOCK] = errors
        out_ref[piece, CORES * BLOCK :] = share


def turn_kernel(core_ref, packed_ref, basis_ref, other_ref, starts_ref, out_ref, share_ref):
    rows = basis_ref.shape[1]
    turned = 0.0
    for core, ref in ((core_ref[0], basis_ref), (1 - core_ref[0], other_ref)):
        errors = packed_ref[:, pl.ds(pl.multiple_of(core * BLOCK, BLOCK), BLOCK), :].reshape(PARTS * BLOCK, LANES)
        turned += lax.dot_general(
            errors[:, :rows], ref[0], (((1,), (1,)), ((), ())), preferred_element_type=jnp.float32
        )
    out_ref[:, :, :rows] = turned.astype(jnp.bfloat16).reshape(CHIPS, GROUP, rows)
    out_ref[:, :, rows:] = jnp.zeros((CHIPS, GROUP, LANES - rows), jnp.bfloat16)
    dealt = packed_ref[:, CORES * BLOCK :, :].reshape(PARTS * CORES * SHARE, LANES)
    order = pick((GROUP, PARTS * CORES * SHARE), lambda row: row // DEALT * SHARE + lax.rem(row, DEALT))
    share = jnp.dot(order, dealt, preferred_element_type=jnp.float32).astype(jnp.bfloat16)
    for piece in range(PARTS):
        share_ref[piece] = share


def sum_kernel(pieces_ref, out_ref):
    out_ref[...] = jnp.sum(pieces_ref[...].astype(jnp.float32), axis=0).astype(jnp.bfloat16)


def gradient_kernel(starts_ref, turned_ref, projected_ref, out_ref, total_ref):
    for sequence in range(SEQS):
        start, end = starts_ref[sequence], starts_ref[sequence + 1]
        begin = pl.multiple_of(jnp.minimum(start // 16 * 16, TOKENS - WINDOW), 16)
        token = begin + lax.broadcasted_iota(jnp.int32, (WINDOW, 1), 0)
        member = (token >= start) & (token < end)
        turned = turned_ref[pl.ds(begin, WINDOW), :]
        turned = jnp.where(member, turned, jnp.zeros((), jnp.bfloat16))
        gradient = lax.dot_general(
            turned,
            projected_ref[pl.ds(begin, WINDOW), :],
            (((0,), (0,)), ((), ())),
            preferred_element_type=jnp.float32,
        )
        if sequence == 0:
            total_ref[...] = gradient * gradient
        elif sequence < SEQS - 1:
            total_ref[...] += gradient * gradient
        else:
            out_ref[...] = (total_ref[...] + gradient * gradient).reshape(out_ref.shape)


def gradients(starts, turned, projected, height):
    width = projected.shape[1]
    tile = 256
    out = pl.pallas_call(
        gradient_kernel,
        out_shape=jax.ShapeDtypeStruct((height, 1, width), jnp.float32),
        grid_spec=pltpu.PrefetchScalarGridSpec(
            num_scalar_prefetch=1,
            grid=(LANES // tile,),
            in_specs=[
                pl.BlockSpec((TOKENS, tile), lambda g, starts: (0, g)),
                pl.BlockSpec((TOKENS, width), lambda g, starts: (0, 0)),
            ],
            out_specs=pl.BlockSpec((tile, 1, width), lambda g, starts: (g, 0, 0)),
            scratch_shapes=[pltpu.VMEM((tile, width), jnp.float32)],
        ),
        compiler_params=pltpu.CompilerParams(vmem_limit_bytes=16 * 1024 * 1024),
    )(starts, turned, projected)
    return out.transpose(1, 0, 2)


def exchange(values, axis):
    return lax.all_to_all(values, axis, 0, 0, tiled=True)


def swap(values):
    return lax.ppermute(values, "core", [(i, CORES - 1 - i) for i in range(CORES)])


def body(hidden, unembed, rotate_vocab, rotate_width, labels, seq_ids):
    rows = unembed.shape[1]
    vocab, chip, core, width = (lax.axis_index(a).astype(jnp.int32) for a in ("vocab", "chip", "core", "width"))
    place = jnp.stack([core, (vocab * PARTS + chip * CORES) * rows])
    core = core.reshape(1)
    mine = lax.dynamic_slice_in_dim(labels, owned(core[0], width), BLOCK, 0).reshape(BLOCK, 1)
    sequence_index = jnp.arange(SEQS + 1, dtype=jnp.int32)
    starts = jnp.sum((seq_ids[None, :] < sequence_index[:, None]).astype(jnp.int32), axis=1)
    half, single = jnp.bfloat16, jnp.float32

    pieces = partial_sums(vocab.reshape(1), hidden, unembed, rotate_width)
    pieces = exchange(pieces, ("core", "width"))
    logits, stats, keep, send = call(
        functools.partial(local_kernel, rows),
        [
            ((CORES * BLOCK, LANES), single),
            ((PARTS * CHIPS, 2, 128), single),
            ((SHARE, LANES), single),
            ((SHARE, LANES), single),
        ],
        [SCALARS, FULL],
    )(core, pieces)
    stats = exchange(stats, ("vocab", "chip"))
    packed = call(
        functools.partial(error_kernel, rows),
        [((PARTS, CORES * ROWS, LANES), half)],
        [SCALARS, FULL, FULL, FULL, FULL, FULL],
    )(place, logits, stats, mine, keep, swap(send))
    turned, share = call(
        turn_kernel,
        [((CHIPS, GROUP, LANES), half), ((PARTS, GROUP, LANES), half)],
        [SCALARS, FULL, FULL, FULL, pl.BlockSpec(memory_space=pl.ANY)],
    )(core, exchange(packed, "width"), rotate_vocab, swap(rotate_vocab), starts)
    projected = exchange(share, "vocab").reshape(TOKENS, LANES)
    turned = call(sum_kernel, [((GROUP, LANES), half)], [FULL])(exchange(turned, "chip"))
    turned = lax.all_gather(turned, ROW, axis=0, tiled=True)
    return gradients(starts, turned, projected, rows)


def solution(mesh):
    vocab, row, width = mesh.axis_names
    devices = mesh.devices.reshape(PARTS, CHIPS, CORES, PARTS)
    in_specs = (
        P(None, width),
        P(vocab, ROW, width),
        P(vocab, width, ROW),
        P(width, ROW),
        P(),
        P(),
    )
    return jax.shard_map(
        body,
        mesh=Mesh(devices, (vocab, *ROW, width)),
        in_specs=in_specs,
        out_specs=P(vocab, width, ROW),
        check_vma=False,
    )
```

```python
import functools

import jax
import jax.numpy as jnp
from jax import lax
from jax.experimental import pallas as pl
from jax.experimental.pallas import tpu as pltpu
from jax.sharding import Mesh
from jax.sharding import PartitionSpec as P

SEQ_LEN = 128
SEQS = 12
PARTS = 8
CORES = 2
CHIPS = PARTS // CORES
TOKENS = 768
GROUP = TOKENS // PARTS
BLOCK = GROUP // CORES
DEALT = BLOCK // PARTS
SHARE = 8
ROWS = BLOCK + SHARE
PAIRS = BLOCK // 2
LANES = 512
WINDOW = SEQ_LEN + 16
VMEM = 48 * 1024 * 1024
MOST = 60 * 1024 * 1024

FULL = pl.BlockSpec(memory_space=pltpu.VMEM)
SCALARS = pl.BlockSpec(memory_space=pltpu.SMEM)
ROW = ("chip", "core")


def call(kernel, outs, ins):
    shapes = [jax.ShapeDtypeStruct(s, d) for s, d in outs]
    return pl.pallas_call(
        kernel,
        out_shape=shapes if len(shapes) > 1 else shapes[0],
        in_specs=ins,
        out_specs=[FULL] * len(shapes) if len(shapes) > 1 else FULL,
        compiler_params=pltpu.CompilerParams(vmem_limit_bytes=VMEM),
    )


def pick(shape, source):
    row = lax.broadcasted_iota(jnp.int32, shape, 0)
    column = lax.broadcasted_iota(jnp.int32, shape, 1)
    return (column == source(row)).astype(jnp.float32).astype(jnp.bfloat16)


def owned(core, width):
    return (width // CORES * CORES + core) * GROUP + width % CORES * BLOCK


def step_of(exponent):
    return jnp.exp2(exponent)


def encode(values, bits):
    top, low = jnp.max(values, axis=1, keepdims=True), jnp.min(values, axis=1, keepdims=True)
    middle, radius = 0.5 * top + 0.5 * low, 0.5 * top - 0.5 * low
    least = jnp.maximum(radius / (0.97 * 2.0 ** (bits - 1)), jnp.abs(middle) * 2.0**-29)
    exponent = jnp.ceil(jnp.log2(jnp.maximum(least, 2.0**-100)))
    step = step_of(exponent)
    offset = jnp.floor(middle / step + 0.5)
    high = jnp.floor(offset / 32768.0)
    return jnp.floor((values - offset * step) / step + 0.5), (exponent, high, offset - high * 32768.0)


def whole(values):
    return values.astype(jnp.int32).astype(jnp.int16)


def partial_kernel(place_ref, hidden_ref, mine_ref, unembed_ref, width_ref, out_ref):
    rows = unembed_ref.shape[1]
    logits = lax.dot_general(
        hidden_ref[...], unembed_ref[0], (((1,), (1,)), ((), ())), preferred_element_type=jnp.float32
    )

    def source(row):
        core, width, within = row // (PARTS * SHARE), lax.rem(row // SHARE, PARTS), lax.rem(row, SHARE)
        return jnp.where(within < DEALT, (width * CORES + core) * DEALT + within, -1)

    dealt = jnp.dot(pick((CORES * PARTS * SHARE, GROUP), source), mine_ref[...], preferred_element_type=jnp.float32)
    projected = jnp.dot(dealt.astype(jnp.bfloat16), width_ref[...], preferred_element_type=jnp.float32)
    projected, share_notes = encode(projected, 16)
    logits, logit_notes = encode(logits, 24)
    high = jnp.floor(logits / 256.0 + 0.5)
    low = logits - high * 256.0
    lane = lax.broadcasted_iota(jnp.int32, (BLOCK, LANES - rows), 1)
    rest = jnp.zeros((BLOCK - SHARE, 1), jnp.float32)
    for core in range(CORES):
        for width in range(PARTS):
            owner, begin = core * PARTS + width, owned(core, width)
            tokens, shares = slice(begin, begin + BLOCK), slice(owner * SHARE, (owner + 1) * SHARE)
            notes = jnp.zeros((BLOCK, LANES - rows), jnp.float32)
            for number, part in enumerate(logit_notes):
                notes = jnp.where(lane == number, part[tokens], notes)
            for number, part in enumerate(share_notes):
                notes = jnp.where(lane == 3 + number, jnp.concatenate([part[shares], rest], axis=0), notes)
            out_ref[owner, :BLOCK, :rows] = whole(high[tokens])
            out_ref[owner, :BLOCK, rows:] = whole(notes)
            pairs = low[begin : begin + PAIRS] * 256.0 + (low[begin + PAIRS : begin + BLOCK] + 128.0)
            pairs = jnp.concatenate([pairs, jnp.zeros((PAIRS, LANES - rows), jnp.float32)], axis=1)
            out_ref[owner, BLOCK:, :] = whole(jnp.concatenate([pairs, projected[shares]], axis=0))


def partial_sums(place, hidden, unembed, rotate_width):
    return pl.pallas_call(
        partial_kernel,
        out_shape=jax.ShapeDtypeStruct((CORES * PARTS, ROWS + PAIRS, LANES), jnp.int16),
        grid_spec=pltpu.PrefetchScalarGridSpec(
            num_scalar_prefetch=1,
            grid=(1,),
            in_specs=[
                pl.BlockSpec(hidden.shape, lambda g, place: (0, 0)),
                pl.BlockSpec((GROUP, hidden.shape[1]), lambda g, place: (place[0], 0)),
                pl.BlockSpec(unembed.shape, lambda g, place: (0, 0, 0)),
                pl.BlockSpec(rotate_width.shape, lambda g, place: (0, 0)),
            ],
            out_specs=pl.BlockSpec((CORES * PARTS, ROWS + PAIRS, LANES), lambda g, place: (0, 0, 0)),
        ),
        compiler_params=pltpu.CompilerParams(vmem_limit_bytes=MOST),
    )(place, hidden, hidden, unembed, rotate_width)


def decode(rows, pieces_ref, owner):
    high = pieces_ref[owner, :BLOCK].astype(jnp.int32).astype(jnp.float32)
    rest = pieces_ref[owner, BLOCK:].astype(jnp.int32).astype(jnp.float32)
    notes, pairs, share = high[:, rows:], rest[:PAIRS], rest[PAIRS:]
    first = jnp.floor(pairs / 256.0)
    low = jnp.concatenate([first, pairs - first * 256.0 - 128.0], axis=0)

    def offset(notes):
        return notes[:, 0:1] * 32768.0 + notes[:, 1:2]

    step = step_of(notes[:, 0:1])
    logits = (high * 256.0 + low) * step + offset(notes[:, 1:3]) * step
    step = step_of(notes[:SHARE, 3:4])
    share = share * step + offset(notes[:SHARE, 4:6]) * step
    return jnp.concatenate([logits, share], axis=0)


def local_kernel(rows, core_ref, pieces_ref, logits_ref, stats_ref, keep_ref, send_ref):
    sums = [sum(decode(rows, pieces_ref, core * PARTS + width) for width in range(PARTS)) for core in range(CORES)]
    column = lax.broadcasted_iota(jnp.int32, (CORES * BLOCK, LANES), 1)
    logits = jnp.concatenate([part[:BLOCK] for part in sums], axis=0)
    logits = jnp.where(column < rows, logits, -jnp.inf)
    logits_ref[...] = logits
    first = core_ref[0] == 0
    keep_ref[...] = jnp.where(first, sums[0][BLOCK:], sums[1][BLOCK:])
    send_ref[...] = jnp.where(first, sums[1][BLOCK:], sums[0][BLOCK:])
    largest = jnp.max(logits, axis=1, keepdims=True)
    largest = jnp.maximum(largest[:BLOCK], largest[BLOCK:])
    total = jnp.sum(jnp.exp(logits - jnp.concatenate([largest, largest], axis=0)), axis=1, keepdims=True)
    total = total[:BLOCK] + total[BLOCK:]
    lane = lax.broadcasted_iota(jnp.int32, (BLOCK, 128), 1)
    square = jnp.concatenate(
        [jnp.where(lane == 0, largest, total), jnp.zeros((128 - BLOCK, 128), jnp.float32)], axis=0
    )
    tile = square.T[: stats_ref.shape[1]]
    for device in range(stats_ref.shape[0]):
        stats_ref[device] = tile


def error_kernel(rows, place_ref, logits_ref, stats_ref, labels_ref, keep_ref, got_ref, out_ref):
    largest = jnp.max(stats_ref[:, 0:1, :], axis=0)
    total = jnp.sum(stats_ref[:, 1:2, :] * jnp.exp(stats_ref[:, 0:1, :] - largest[None]), axis=0)
    row = lax.broadcasted_iota(jnp.int32, (128, 128), 0)
    square = jnp.where(row == 0, largest, total).T
    largest, total = square[:BLOCK, 0:1], square[:BLOCK, 1:2]
    column = lax.broadcasted_iota(jnp.int32, (BLOCK, LANES), 1)
    parts = []
    for core in range(CORES):
        probabilities = jnp.exp(logits_ref[core * BLOCK : (core + 1) * BLOCK] - largest) / total
        hit = (labels_ref[...] - (place_ref[1] + core * rows) == column) & (column < rows)
        parts.append((probabilities - hit.astype(jnp.float32)).astype(jnp.bfloat16))
    errors = jnp.concatenate(parts, axis=0)
    first = place_ref[0] == 0
    keep, got = keep_ref[...], got_ref[...]
    share = jnp.concatenate([jnp.where(first, keep, got), jnp.where(first, got, keep)], axis=0).astype(jnp.bfloat16)
    for piece in range(PARTS):
        out_ref[piece, : CORES * BLOCK] = errors
        out_ref[piece, CORES * BLOCK :] = share


def turn_kernel(core_ref, packed_ref, basis_ref, other_ref, starts_ref, out_ref, share_ref):
    rows = basis_ref.shape[1]
    turned = 0.0
    for core, ref in ((core_ref[0], basis_ref), (1 - core_ref[0], other_ref)):
        errors = packed_ref[:, pl.ds(pl.multiple_of(core * BLOCK, BLOCK), BLOCK), :].reshape(PARTS * BLOCK, LANES)
        turned += lax.dot_general(
            errors[:, :rows], ref[0], (((1,), (1,)), ((), ())), preferred_element_type=jnp.float32
        )
    out_ref[:, :, :rows] = turned.astype(jnp.bfloat16).reshape(CHIPS, GROUP, rows)
    out_ref[:, :, rows:] = jnp.zeros((CHIPS, GROUP, LANES - rows), jnp.bfloat16)
    dealt = packed_ref[:, CORES * BLOCK :, :].reshape(PARTS * CORES * SHARE, LANES)
    order = pick((GROUP, PARTS * CORES * SHARE), lambda row: row // DEALT * SHARE + lax.rem(row, DEALT))
    share = jnp.dot(order, dealt, preferred_element_type=jnp.float32).astype(jnp.bfloat16)
    for piece in range(PARTS):
        share_ref[piece] = share


def sum_kernel(pieces_ref, out_ref):
    out_ref[...] = jnp.sum(pieces_ref[...].astype(jnp.float32), axis=0).astype(jnp.bfloat16)


def gradient_kernel(starts_ref, turned_ref, projected_ref, out_ref, total_ref):
    for sequence in range(SEQS):
        start, end = starts_ref[sequence], starts_ref[sequence + 1]
        begin = pl.multiple_of(jnp.minimum(start // 16 * 16, TOKENS - WINDOW), 16)
        token = begin + lax.broadcasted_iota(jnp.int32, (WINDOW, 1), 0)
        member = (token >= start) & (token < end)
        turned = turned_ref[pl.ds(begin, WINDOW), :]
        turned = jnp.where(member, turned, jnp.zeros((), jnp.bfloat16))
        gradient = lax.dot_general(
            turned,
            projected_ref[pl.ds(begin, WINDOW), :],
            (((0,), (0,)), ((), ())),
            preferred_element_type=jnp.float32,
        )
        if sequence == 0:
            total_ref[...] = gradient * gradient
        elif sequence < SEQS - 1:
            total_ref[...] += gradient * gradient
        else:
            out_ref[...] = (total_ref[...] + gradient * gradient).reshape(out_ref.shape)


def gradients(starts, turned, projected, height):
    width = projected.shape[1]
    tile = 256
    out = pl.pallas_call(
        gradient_kernel,
        out_shape=jax.ShapeDtypeStruct((height, 1, width), jnp.float32),
        grid_spec=pltpu.PrefetchScalarGridSpec(
            num_scalar_prefetch=1,
            grid=(LANES // tile,),
            in_specs=[
                pl.BlockSpec((TOKENS, tile), lambda g, starts: (0, g)),
                pl.BlockSpec((TOKENS, width), lambda g, starts: (0, 0)),
            ],
            out_specs=pl.BlockSpec((tile, 1, width), lambda g, starts: (g, 0, 0)),
            scratch_shapes=[pltpu.VMEM((tile, width), jnp.float32)],
        ),
        compiler_params=pltpu.CompilerParams(vmem_limit_bytes=16 * 1024 * 1024),
    )(starts, turned, projected)
    return out.transpose(1, 0, 2)


def exchange(values, axis):
    return lax.all_to_all(values, axis, 0, 0, tiled=True)


def swap(values):
    return lax.ppermute(values, "core", [(i, CORES - 1 - i) for i in range(CORES)])


def body(hidden, unembed, rotate_vocab, rotate_width, labels, seq_ids):
    rows = unembed.shape[1]
    vocab, chip, core, width = (lax.axis_index(a).astype(jnp.int32) for a in ("vocab", "chip", "core", "width"))
    place = jnp.stack([core, (vocab * PARTS + chip * CORES) * rows])
    core = core.reshape(1)
    mine = lax.dynamic_slice_in_dim(labels, owned(core[0], width), BLOCK, 0).reshape(BLOCK, 1)
    sequence_index = jnp.arange(SEQS + 1, dtype=jnp.int32)
    starts = jnp.sum((seq_ids[None, :] < sequence_index[:, None]).astype(jnp.int32), axis=1)
    half, single = jnp.bfloat16, jnp.float32

    pieces = partial_sums(vocab.reshape(1), hidden, unembed, rotate_width)
    pieces = exchange(pieces, ("core", "width"))
    logits, stats, keep, send = call(
        functools.partial(local_kernel, rows),
        [
            ((CORES * BLOCK, LANES), single),
            ((PARTS * CHIPS, 2, 128), single),
            ((SHARE, LANES), single),
            ((SHARE, LANES), single),
        ],
        [SCALARS, FULL],
    )(core, pieces)
    stats = exchange(stats, ("vocab", "chip"))
    packed = call(
        functools.partial(error_kernel, rows),
        [((PARTS, CORES * ROWS, LANES), half)],
        [SCALARS, FULL, FULL, FULL, FULL, FULL],
    )(place, logits, stats, mine, keep, swap(send))
    turned, share = call(
        turn_kernel,
        [((CHIPS, GROUP, LANES), half), ((PARTS, GROUP, LANES), half)],
        [SCALARS, FULL, FULL, FULL, pl.BlockSpec(memory_space=pl.ANY)],
    )(core, exchange(packed, "width"), rotate_vocab, swap(rotate_vocab), starts)
    projected = exchange(share, "vocab").reshape(TOKENS, LANES)
    turned = call(sum_kernel, [((GROUP, LANES), half)], [FULL])(exchange(turned, "chip"))
    turned = lax.all_gather(turned, ROW, axis=0, tiled=True)
    return gradients(starts, turned, projected, rows)


def solution(mesh):
    vocab, row, width = mesh.axis_names
    devices = mesh.devices.reshape(PARTS, CHIPS, CORES, PARTS)
    in_specs = (
        P(None, width),
        P(vocab, ROW, width),
        P(vocab, width, ROW),
        P(width, ROW),
        P(),
        P(),
    )
    return jax.shard_map(
        body,
        mesh=Mesh(devices, (vocab, *ROW, width)),
        in_specs=in_specs,
        out_specs=P(vocab, width, ROW),
        check_vma=False,
    )
```

```python
import functools

import jax
import jax.numpy as jnp
from jax import lax
from jax.experimental import pallas as pl
from jax.experimental.pallas import tpu as pltpu
from jax.sharding import Mesh
from jax.sharding import PartitionSpec as P

SEQ_LEN = 128
SEQS = 12
PARTS = 8
CORES = 2
CHIPS = PARTS // CORES
TOKENS = 768
GROUP = TOKENS // PARTS
BLOCK = GROUP // CORES
DEALT = BLOCK // PARTS
SHARE = 8
ROWS = BLOCK + SHARE
PAIRS = BLOCK // 2
LANES = 512
WINDOW = SEQ_LEN + 16
VMEM = 48 * 1024 * 1024
MOST = 60 * 1024 * 1024

FULL = pl.BlockSpec(memory_space=pltpu.VMEM)
SCALARS = pl.BlockSpec(memory_space=pltpu.SMEM)
ROW = ("chip", "core")


def call(kernel, outs, ins):
    shapes = [jax.ShapeDtypeStruct(s, d) for s, d in outs]
    return pl.pallas_call(
        kernel,
        out_shape=shapes if len(shapes) > 1 else shapes[0],
        in_specs=ins,
        out_specs=[FULL] * len(shapes) if len(shapes) > 1 else FULL,
        compiler_params=pltpu.CompilerParams(vmem_limit_bytes=VMEM),
    )


def pick(shape, source):
    row = lax.broadcasted_iota(jnp.int32, shape, 0)
    column = lax.broadcasted_iota(jnp.int32, shape, 1)
    return (column == source(row)).astype(jnp.float32).astype(jnp.bfloat16)


def owned(core, width):
    return (width // CORES * CORES + core) * GROUP + width % CORES * BLOCK


def step_of(exponent):
    return jnp.exp2(exponent)


def encode(values, bits):
    top, low = jnp.max(values, axis=1, keepdims=True), jnp.min(values, axis=1, keepdims=True)
    middle, radius = 0.5 * top + 0.5 * low, 0.5 * top - 0.5 * low
    least = jnp.maximum(radius / (0.97 * 2.0 ** (bits - 1)), jnp.abs(middle) * 2.0**-29)
    exponent = jnp.ceil(jnp.log2(jnp.maximum(least, 2.0**-100)))
    step = step_of(exponent)
    offset = jnp.floor(middle / step + 0.5)
    high = jnp.floor(offset / 32768.0)
    return jnp.floor((values - offset * step) / step + 0.5), (exponent, high, offset - high * 32768.0)


def whole(values):
    return values.astype(jnp.int32).astype(jnp.int16)


def partial_kernel(place_ref, hidden_ref, mine_ref, unembed_ref, width_ref, out_ref):
    rows = unembed_ref.shape[1]
    logits = lax.dot_general(
        hidden_ref[...], unembed_ref[0], (((1,), (1,)), ((), ())), preferred_element_type=jnp.float32
    )

    def source(row):
        core, width, within = row // (PARTS * SHARE), lax.rem(row // SHARE, PARTS), lax.rem(row, SHARE)
        return jnp.where(within < DEALT, (width * CORES + core) * DEALT + within, -1)

    dealt = jnp.dot(pick((CORES * PARTS * SHARE, GROUP), source), mine_ref[...], preferred_element_type=jnp.float32)
    projected = jnp.dot(dealt.astype(jnp.bfloat16), width_ref[...], preferred_element_type=jnp.float32)
    projected, share_notes = encode(projected, 16)
    logits, logit_notes = encode(logits, 24)
    high = jnp.floor(logits / 256.0 + 0.5)
    low = logits - high * 256.0
    lane = lax.broadcasted_iota(jnp.int32, (BLOCK, LANES - rows), 1)
    rest = jnp.zeros((BLOCK - SHARE, 1), jnp.float32)
    for core in range(CORES):
        for width in range(PARTS):
            owner, begin = core * PARTS + width, owned(core, width)
            tokens, shares = slice(begin, begin + BLOCK), slice(owner * SHARE, (owner + 1) * SHARE)
            notes = jnp.zeros((BLOCK, LANES - rows), jnp.float32)
            for number, part in enumerate(logit_notes):
                notes = jnp.where(lane == number, part[tokens], notes)
            for number, part in enumerate(share_notes):
                notes = jnp.where(lane == 3 + number, jnp.concatenate([part[shares], rest], axis=0), notes)
            out_ref[owner, :BLOCK, :rows] = whole(high[tokens])
            out_ref[owner, :BLOCK, rows:] = whole(notes)
            pairs = low[begin : begin + PAIRS] * 256.0 + (low[begin + PAIRS : begin + BLOCK] + 128.0)
            pairs = jnp.concatenate([pairs, jnp.zeros((PAIRS, LANES - rows), jnp.float32)], axis=1)
            out_ref[owner, BLOCK:, :] = whole(jnp.concatenate([pairs, projected[shares]], axis=0))


def partial_sums(place, hidden, unembed, rotate_width):
    return pl.pallas_call(
        partial_kernel,
        out_shape=jax.ShapeDtypeStruct((CORES * PARTS, ROWS + PAIRS, LANES), jnp.int16),
        grid_spec=pltpu.PrefetchScalarGridSpec(
            num_scalar_prefetch=1,
            grid=(1,),
            in_specs=[
                pl.BlockSpec(hidden.shape, lambda g, place: (0, 0)),
                pl.BlockSpec((GROUP, hidden.shape[1]), lambda g, place: (place[0], 0)),
                pl.BlockSpec(unembed.shape, lambda g, place: (0, 0, 0)),
                pl.BlockSpec(rotate_width.shape, lambda g, place: (0, 0)),
            ],
            out_specs=pl.BlockSpec((CORES * PARTS, ROWS + PAIRS, LANES), lambda g, place: (0, 0, 0)),
        ),
        compiler_params=pltpu.CompilerParams(vmem_limit_bytes=MOST),
    )(place, hidden, hidden, unembed, rotate_width)


def decode(rows, pieces_ref, owner):
    high = pieces_ref[owner, :BLOCK].astype(jnp.int32).astype(jnp.float32)
    rest = pieces_ref[owner, BLOCK:].astype(jnp.int32).astype(jnp.float32)
    notes, pairs, share = high[:, rows:], rest[:PAIRS], rest[PAIRS:]
    first = jnp.floor(pairs / 256.0)
    low = jnp.concatenate([first, pairs - first * 256.0 - 128.0], axis=0)

    def offset(notes):
        return notes[:, 0:1] * 32768.0 + notes[:, 1:2]

    step = step_of(notes[:, 0:1])
    logits = (high * 256.0 + low) * step + offset(notes[:, 1:3]) * step
    step = step_of(notes[:SHARE, 3:4])
    share = share * step + offset(notes[:SHARE, 4:6]) * step
    return jnp.concatenate([logits, share], axis=0)


def local_kernel(rows, pieces_ref, logits_ref, stats_ref, share_ref):
    sums = [sum(decode(rows, pieces_ref, core * PARTS + width) for width in range(PARTS)) for core in range(CORES)]
    column = lax.broadcasted_iota(jnp.int32, (CORES * BLOCK, LANES), 1)
    logits = jnp.concatenate([part[:BLOCK] for part in sums], axis=0)
    logits = jnp.where(column < rows, logits, -jnp.inf)
    logits_ref[...] = logits
    share_ref[...] = jnp.concatenate([part[BLOCK:] for part in sums], axis=0).astype(jnp.bfloat16)
    largest = jnp.max(logits, axis=1, keepdims=True)
    largest = jnp.maximum(largest[:BLOCK], largest[BLOCK:])
    total = jnp.sum(jnp.exp(logits - jnp.concatenate([largest, largest], axis=0)), axis=1, keepdims=True)
    total = total[:BLOCK] + total[BLOCK:]
    lane = lax.broadcasted_iota(jnp.int32, (BLOCK, 128), 1)
    square = jnp.concatenate(
        [jnp.where(lane == 0, largest, total), jnp.zeros((128 - BLOCK, 128), jnp.float32)], axis=0
    )
    tile = square.T[: stats_ref.shape[1]]
    for device in range(stats_ref.shape[0]):
        stats_ref[device] = tile


def merge_kernel(stats_ref, out_ref):
    largest = jnp.max(stats_ref[:, 0:1, :], axis=0)
    total = jnp.sum(stats_ref[:, 1:2, :] * jnp.exp(stats_ref[:, 0:1, :] - largest[None]), axis=0)
    out_ref[0] = jnp.concatenate([largest, total], axis=0)


def error_kernel(rows, first_ref, logits_ref, stats_ref, labels_ref, share_ref, out_ref):
    largest = jnp.max(stats_ref[:, 0:1, :], axis=0)
    total = jnp.sum(stats_ref[:, 1:2, :] * jnp.exp(stats_ref[:, 0:1, :] - largest[None]), axis=0)
    row = lax.broadcasted_iota(jnp.int32, (128, 128), 0)
    square = jnp.where(row == 0, largest, total).T
    largest, total = square[:BLOCK, 0:1], square[:BLOCK, 1:2]
    column = lax.broadcasted_iota(jnp.int32, (BLOCK, LANES), 1)
    parts = []
    for core in range(CORES):
        probabilities = jnp.exp(logits_ref[core * BLOCK : (core + 1) * BLOCK] - largest) / total
        hit = (labels_ref[...] - (first_ref[0] + core * rows) == column) & (column < rows)
        parts.append((probabilities - hit.astype(jnp.float32)).astype(jnp.bfloat16))
    errors = jnp.concatenate(parts, axis=0)
    for piece in range(PARTS):
        out_ref[piece, : CORES * BLOCK] = errors
        out_ref[piece, CORES * BLOCK :] = share_ref[...]


def turn_kernel(core_ref, packed_ref, basis_ref, other_ref, starts_ref, out_ref, keep_ref, send_ref):
    rows = basis_ref.shape[1]
    turned = 0.0
    for core, ref in ((core_ref[0], basis_ref), (1 - core_ref[0], other_ref)):
        errors = packed_ref[:, pl.ds(pl.multiple_of(core * BLOCK, BLOCK), BLOCK), :].reshape(PARTS * BLOCK, LANES)
        turned += lax.dot_general(
            errors[:, :rows], ref[0], (((1,), (1,)), ((), ())), preferred_element_type=jnp.float32
        )
    out_ref[:, :, :rows] = turned.astype(jnp.bfloat16).reshape(CHIPS, GROUP, rows)
    out_ref[:, :, rows:] = jnp.zeros((CHIPS, GROUP, LANES - rows), jnp.bfloat16)
    share = packed_ref[:, GROUP:, :].astype(jnp.float32)
    first, second = share[:, :SHARE], share[:, SHARE:]
    first_core = core_ref[0] == 0
    keep, send = jnp.where(first_core, first, second), jnp.where(first_core, second, first)
    keep_ref[...] = keep.reshape(PARTS * SHARE, LANES).astype(jnp.bfloat16)
    send_ref[...] = send.reshape(PARTS * SHARE, LANES).astype(jnp.bfloat16)


def share_kernel(core_ref, keep_ref, got_ref, out_ref):
    def order(core):
        def source(row):
            owner, within = row // DEALT, lax.rem(row, DEALT)
            return jnp.where(lax.rem(owner, CORES) == core, owner // CORES * SHARE + within, -1)

        return pick((GROUP, PARTS * SHARE), source)

    core = core_ref[0]
    share = jnp.dot(order(core), keep_ref[...], preferred_element_type=jnp.float32)
    share += jnp.dot(order(1 - core), got_ref[...], preferred_element_type=jnp.float32)
    share = share.astype(jnp.bfloat16)
    for piece in range(PARTS):
        out_ref[piece] = share


def sum_kernel(pieces_ref, out_ref):
    out_ref[...] = jnp.sum(pieces_ref[...].astype(jnp.float32), axis=0).astype(jnp.bfloat16)


def gradient_kernel(starts_ref, turned_ref, projected_ref, out_ref, total_ref):
    for sequence in range(SEQS):
        start, end = starts_ref[sequence], starts_ref[sequence + 1]
        begin = pl.multiple_of(jnp.minimum(start // 16 * 16, TOKENS - WINDOW), 16)
        token = begin + lax.broadcasted_iota(jnp.int32, (WINDOW, 1), 0)
        member = (token >= start) & (token < end)
        turned = turned_ref[pl.ds(begin, WINDOW), :]
        turned = jnp.where(member, turned, jnp.zeros((), jnp.bfloat16))
        gradient = lax.dot_general(
            turned,
            projected_ref[pl.ds(begin, WINDOW), :],
            (((0,), (0,)), ((), ())),
            preferred_element_type=jnp.float32,
        )
        if sequence == 0:
            total_ref[...] = gradient * gradient
        elif sequence < SEQS - 1:
            total_ref[...] += gradient * gradient
        else:
            out_ref[...] = (total_ref[...] + gradient * gradient).reshape(out_ref.shape)


def gradients(starts, turned, projected, height):
    width = projected.shape[1]
    tile = 256
    out = pl.pallas_call(
        gradient_kernel,
        out_shape=jax.ShapeDtypeStruct((height, 1, width), jnp.float32),
        grid_spec=pltpu.PrefetchScalarGridSpec(
            num_scalar_prefetch=1,
            grid=(LANES // tile,),
            in_specs=[
                pl.BlockSpec((TOKENS, tile), lambda g, starts: (0, g)),
                pl.BlockSpec((TOKENS, width), lambda g, starts: (0, 0)),
            ],
            out_specs=pl.BlockSpec((tile, 1, width), lambda g, starts: (g, 0, 0)),
            scratch_shapes=[pltpu.VMEM((tile, width), jnp.float32)],
        ),
        compiler_params=pltpu.CompilerParams(vmem_limit_bytes=16 * 1024 * 1024),
    )(starts, turned, projected)
    return out.transpose(1, 0, 2)


def exchange(values, axis):
    return lax.all_to_all(values, axis, 0, 0, tiled=True)


def swap(values):
    return lax.ppermute(values, "core", [(i, CORES - 1 - i) for i in range(CORES)])


def body(hidden, unembed, rotate_vocab, rotate_width, labels, seq_ids):
    rows = unembed.shape[1]
    vocab, chip, core, width = (lax.axis_index(a).astype(jnp.int32) for a in ("vocab", "chip", "core", "width"))
    first = ((vocab * PARTS + chip * CORES) * rows).reshape(1)
    core = core.reshape(1)
    mine = lax.dynamic_slice_in_dim(labels, owned(core[0], width), BLOCK, 0).reshape(BLOCK, 1)
    sequence_index = jnp.arange(SEQS + 1, dtype=jnp.int32)
    starts = jnp.sum((seq_ids[None, :] < sequence_index[:, None]).astype(jnp.int32), axis=1)
    half, single = jnp.bfloat16, jnp.float32

    pieces = partial_sums(vocab.reshape(1), hidden, unembed, rotate_width)
    pieces = exchange(pieces, ("core", "width"))
    logits, stats, share = call(
        functools.partial(local_kernel, rows),
        [((GROUP, LANES), single), ((1, 2, 128), single), ((CORES * SHARE, LANES), half)],
        [FULL],
    )(pieces)
    stats = lax.all_gather(stats, "vocab", axis=0, tiled=True)
    stats = call(merge_kernel, [((1, 2, 128), single)], [FULL])(stats)
    stats = lax.all_gather(stats, "chip", axis=0, tiled=True)
    packed = call(
        functools.partial(error_kernel, rows),
        [((PARTS, CORES * ROWS, LANES), half)],
        [SCALARS, FULL, FULL, FULL, FULL],
    )(first, logits, stats, mine, share)
    turned, keep, send = call(
        turn_kernel,
        [((CHIPS, GROUP, LANES), half), ((PARTS * SHARE, LANES), half), ((PARTS * SHARE, LANES), half)],
        [SCALARS, FULL, FULL, FULL, pl.BlockSpec(memory_space=pl.ANY)],
    )(core, exchange(packed, "width"), rotate_vocab, swap(rotate_vocab), starts)
    share = call(share_kernel, [((PARTS, GROUP, LANES), half)], [SCALARS, FULL, FULL])(core, keep, swap(send))
    projected = exchange(share, "vocab").reshape(TOKENS, LANES)
    turned = call(sum_kernel, [((GROUP, LANES), half)], [FULL])(exchange(turned, "chip"))
    turned = lax.all_gather(turned, ROW, axis=0, tiled=True)
    return gradients(starts, turned, projected, rows)


def solution(mesh):
    vocab, row, width = mesh.axis_names
    devices = mesh.devices.reshape(PARTS, CHIPS, CORES, PARTS)
    in_specs = (
        P(None, width),
        P(vocab, ROW, width),
        P(vocab, width, ROW),
        P(width, ROW),
        P(),
        P(),
    )
    return jax.shard_map(
        body,
        mesh=Mesh(devices, (vocab, *ROW, width)),
        in_specs=in_specs,
        out_specs=P(vocab, width, ROW),
        check_vma=False,
    )
```

```python
import functools

import jax
import jax.numpy as jnp
from jax import lax
from jax.experimental import pallas as pl
from jax.experimental.pallas import tpu as pltpu
from jax.sharding import Mesh
from jax.sharding import PartitionSpec as P

SEQ_LEN = 128
SEQS = 12
PARTS = 8
CORES = 2
CHIPS = PARTS // CORES
TOKENS = 768
GROUP = TOKENS // PARTS
BLOCK = GROUP // CORES
DEALT = BLOCK // PARTS
SHARE = 8
ROWS = BLOCK + SHARE
PAIRS = BLOCK // 2
LANES = 512
CHUNKS = 2
WINDOW = SEQ_LEN + 16
VMEM = 48 * 1024 * 1024
MOST = 60 * 1024 * 1024

FULL = pl.BlockSpec(memory_space=pltpu.VMEM)
SCALARS = pl.BlockSpec(memory_space=pltpu.SMEM)
ROW = ("chip", "core")


def call(kernel, outs, ins):
    shapes = [jax.ShapeDtypeStruct(s, d) for s, d in outs]
    return pl.pallas_call(
        kernel,
        out_shape=shapes if len(shapes) > 1 else shapes[0],
        in_specs=ins,
        out_specs=[FULL] * len(shapes) if len(shapes) > 1 else FULL,
        compiler_params=pltpu.CompilerParams(vmem_limit_bytes=VMEM),
    )


def pick(shape, source):
    row = lax.broadcasted_iota(jnp.int32, shape, 0)
    column = lax.broadcasted_iota(jnp.int32, shape, 1)
    return (column == source(row)).astype(jnp.float32).astype(jnp.bfloat16)


def owned(core, width):
    return (width // CORES * CORES + core) * GROUP + width % CORES * BLOCK


def step_of(exponent):
    return jnp.exp2(exponent)


def encode(values, bits):
    top, low = jnp.max(values, axis=1, keepdims=True), jnp.min(values, axis=1, keepdims=True)
    middle, radius = 0.5 * top + 0.5 * low, 0.5 * top - 0.5 * low
    least = jnp.maximum(radius / (0.97 * 2.0 ** (bits - 1)), jnp.abs(middle) * 2.0**-29)
    exponent = jnp.ceil(jnp.log2(jnp.maximum(least, 2.0**-100)))
    step = step_of(exponent)
    offset = jnp.floor(middle / step + 0.5)
    high = jnp.floor(offset / 32768.0)
    return jnp.floor((values - offset * step) / step + 0.5), (exponent, high, offset - high * 32768.0)


def whole(values):
    return values.astype(jnp.int32).astype(jnp.int16)


def partial_kernel(
    place_ref, hidden_hbm, unembed_hbm, width_hbm, out_ref, hidden_ref, unembed_ref, width_ref, logits_ref, sems
):
    rows = unembed_ref.shape[1]
    chunk = TOKENS // CHUNKS
    copies = [pltpu.make_async_copy(unembed_hbm, unembed_ref, sems.at[CHUNKS])]
    for number in range(CHUNKS):
        part = pl.ds(number * chunk, chunk)
        copies.append(pltpu.make_async_copy(hidden_hbm.at[part], hidden_ref.at[part], sems.at[number]))
    copies.append(pltpu.make_async_copy(width_hbm, width_ref, sems.at[CHUNKS + 1]))
    for copy in copies:
        copy.start()
    copies[0].wait()
    for number in range(CHUNKS):
        copies[1 + number].wait()
        part = slice(number * chunk, (number + 1) * chunk)
        logits_ref[part] = lax.dot_general(
            hidden_ref[part], unembed_ref[0], (((1,), (1,)), ((), ())), preferred_element_type=jnp.float32
        )
    copies[-1].wait()
    logits = logits_ref[...]
    mine = hidden_ref[pl.ds(pl.multiple_of(place_ref[0] * GROUP, GROUP), GROUP), :]

    def source(row):
        core, width, within = row // (PARTS * SHARE), lax.rem(row // SHARE, PARTS), lax.rem(row, SHARE)
        return jnp.where(within < DEALT, (width * CORES + core) * DEALT + within, -1)

    dealt = jnp.dot(pick((CORES * PARTS * SHARE, GROUP), source), mine, preferred_element_type=jnp.float32)
    projected = jnp.dot(dealt.astype(jnp.bfloat16), width_ref[...], preferred_element_type=jnp.float32)
    projected, share_notes = encode(projected, 16)
    logits, logit_notes = encode(logits, 24)
    high = jnp.floor(logits / 256.0 + 0.5)
    low = logits - high * 256.0
    lane = lax.broadcasted_iota(jnp.int32, (BLOCK, LANES - rows), 1)
    rest = jnp.zeros((BLOCK - SHARE, 1), jnp.float32)
    for core in range(CORES):
        for width in range(PARTS):
            owner, begin = core * PARTS + width, owned(core, width)
            tokens, shares = slice(begin, begin + BLOCK), slice(owner * SHARE, (owner + 1) * SHARE)
            notes = jnp.zeros((BLOCK, LANES - rows), jnp.float32)
            for number, part in enumerate(logit_notes):
                notes = jnp.where(lane == number, part[tokens], notes)
            for number, part in enumerate(share_notes):
                notes = jnp.where(lane == 3 + number, jnp.concatenate([part[shares], rest], axis=0), notes)
            out_ref[owner, :BLOCK, :rows] = whole(high[tokens])
            out_ref[owner, :BLOCK, rows:] = whole(notes)
            pairs = low[begin : begin + PAIRS] * 256.0 + (low[begin + PAIRS : begin + BLOCK] + 128.0)
            pairs = jnp.concatenate([pairs, jnp.zeros((PAIRS, LANES - rows), jnp.float32)], axis=1)
            out_ref[owner, BLOCK:, :] = whole(jnp.concatenate([pairs, projected[shares]], axis=0))


def partial_sums(place, hidden, unembed, rotate_width):
    anywhere = pl.BlockSpec(memory_space=pl.ANY)
    return pl.pallas_call(
        partial_kernel,
        out_shape=jax.ShapeDtypeStruct((CORES * PARTS, ROWS + PAIRS, LANES), jnp.int16),
        in_specs=[SCALARS, anywhere, anywhere, anywhere],
        out_specs=FULL,
        scratch_shapes=[
            pltpu.VMEM(hidden.shape, hidden.dtype),
            pltpu.VMEM(unembed.shape, unembed.dtype),
            pltpu.VMEM(rotate_width.shape, rotate_width.dtype),
            pltpu.VMEM((TOKENS, unembed.shape[1]), jnp.float32),
            pltpu.SemaphoreType.DMA((CHUNKS + 2,)),
        ],
        compiler_params=pltpu.CompilerParams(vmem_limit_bytes=MOST),
    )(place, hidden, unembed, rotate_width)


def decode(rows, pieces_ref, owner):
    high = pieces_ref[owner, :BLOCK].astype(jnp.int32).astype(jnp.float32)
    rest = pieces_ref[owner, BLOCK:].astype(jnp.int32).astype(jnp.float32)
    notes, pairs, share = high[:, rows:], rest[:PAIRS], rest[PAIRS:]
    first = jnp.floor(pairs / 256.0)
    low = jnp.concatenate([first, pairs - first * 256.0 - 128.0], axis=0)

    def offset(notes):
        return notes[:, 0:1] * 32768.0 + notes[:, 1:2]

    step = step_of(notes[:, 0:1])
    logits = (high * 256.0 + low) * step + offset(notes[:, 1:3]) * step
    step = step_of(notes[:SHARE, 3:4])
    share = share * step + offset(notes[:SHARE, 4:6]) * step
    return jnp.concatenate([logits, share], axis=0)


def local_kernel(rows, pieces_ref, unread_ref, logits_ref, stats_ref, share_ref):
    sums = [sum(decode(rows, pieces_ref, core * PARTS + width) for width in range(PARTS)) for core in range(CORES)]
    column = lax.broadcasted_iota(jnp.int32, (CORES * BLOCK, LANES), 1)
    logits = jnp.concatenate([part[:BLOCK] for part in sums], axis=0)
    logits = jnp.where(column < rows, logits, -jnp.inf)
    logits_ref[...] = logits
    share_ref[...] = jnp.concatenate([part[BLOCK:] for part in sums], axis=0).astype(jnp.bfloat16)
    largest = jnp.max(logits, axis=1, keepdims=True)
    largest = jnp.maximum(largest[:BLOCK], largest[BLOCK:])
    total = jnp.sum(jnp.exp(logits - jnp.concatenate([largest, largest], axis=0)), axis=1, keepdims=True)
    total = total[:BLOCK] + total[BLOCK:]
    lane = lax.broadcasted_iota(jnp.int32, (BLOCK, 128), 1)
    square = jnp.concatenate(
        [jnp.where(lane == 0, largest, total), jnp.zeros((128 - BLOCK, 128), jnp.float32)], axis=0
    )
    tile = square.T[: stats_ref.shape[1]]
    for device in range(stats_ref.shape[0]):
        stats_ref[device] = tile


def merge_kernel(stats_ref, out_ref):
    largest = jnp.max(stats_ref[:, 0:1, :], axis=0)
    total = jnp.sum(stats_ref[:, 1:2, :] * jnp.exp(stats_ref[:, 0:1, :] - largest[None]), axis=0)
    out_ref[0] = jnp.concatenate([largest, total], axis=0)


def error_kernel(rows, first_ref, logits_ref, stats_ref, labels_ref, share_ref, out_ref):
    largest = jnp.max(stats_ref[:, 0:1, :], axis=0)
    total = jnp.sum(stats_ref[:, 1:2, :] * jnp.exp(stats_ref[:, 0:1, :] - largest[None]), axis=0)
    row = lax.broadcasted_iota(jnp.int32, (128, 128), 0)
    square = jnp.where(row == 0, largest, total).T
    largest, total = square[:BLOCK, 0:1], square[:BLOCK, 1:2]
    column = lax.broadcasted_iota(jnp.int32, (BLOCK, LANES), 1)
    parts = []
    for core in range(CORES):
        probabilities = jnp.exp(logits_ref[core * BLOCK : (core + 1) * BLOCK] - largest) / total
        hit = (labels_ref[...] - (first_ref[0] + core * rows) == column) & (column < rows)
        parts.append((probabilities - hit.astype(jnp.float32)).astype(jnp.bfloat16))
    errors = jnp.concatenate(parts, axis=0)
    for piece in range(PARTS):
        out_ref[piece, : CORES * BLOCK] = errors
        out_ref[piece, CORES * BLOCK :] = share_ref[...]


def turn_kernel(core_ref, packed_ref, basis_ref, other_ref, starts_ref, out_ref, keep_ref, send_ref):
    rows = basis_ref.shape[1]
    turned = 0.0
    for core, ref in ((core_ref[0], basis_ref), (1 - core_ref[0], other_ref)):
        errors = packed_ref[:, pl.ds(pl.multiple_of(core * BLOCK, BLOCK), BLOCK), :].reshape(PARTS * BLOCK, LANES)
        turned += lax.dot_general(
            errors[:, :rows], ref[0], (((1,), (1,)), ((), ())), preferred_element_type=jnp.float32
        )
    out_ref[:, :, :rows] = turned.astype(jnp.bfloat16).reshape(CHIPS, GROUP, rows)
    out_ref[:, :, rows:] = jnp.zeros((CHIPS, GROUP, LANES - rows), jnp.bfloat16)
    share = packed_ref[:, GROUP:, :].astype(jnp.float32)
    first, second = share[:, :SHARE], share[:, SHARE:]
    first_core = core_ref[0] == 0
    keep, send = jnp.where(first_core, first, second), jnp.where(first_core, second, first)
    keep_ref[...] = keep.reshape(PARTS * SHARE, LANES).astype(jnp.bfloat16)
    send_ref[...] = send.reshape(PARTS * SHARE, LANES).astype(jnp.bfloat16)


def share_kernel(core_ref, keep_ref, got_ref, out_ref):
    def order(core):
        def source(row):
            owner, within = row // DEALT, lax.rem(row, DEALT)
            return jnp.where(lax.rem(owner, CORES) == core, owner // CORES * SHARE + within, -1)

        return pick((GROUP, PARTS * SHARE), source)

    core = core_ref[0]
    share = jnp.dot(order(core), keep_ref[...], preferred_element_type=jnp.float32)
    share += jnp.dot(order(1 - core), got_ref[...], preferred_element_type=jnp.float32)
    share = share.astype(jnp.bfloat16)
    for piece in range(PARTS):
        out_ref[piece] = share


def sum_kernel(pieces_ref, out_ref):
    out_ref[...] = jnp.sum(pieces_ref[...].astype(jnp.float32), axis=0).astype(jnp.bfloat16)


def gradient_kernel(starts_ref, turned_ref, projected_ref, out_ref, total_ref):
    for sequence in range(SEQS):
        start, end = starts_ref[sequence], starts_ref[sequence + 1]
        begin = pl.multiple_of(jnp.minimum(start // 16 * 16, TOKENS - WINDOW), 16)
        token = begin + lax.broadcasted_iota(jnp.int32, (WINDOW, 1), 0)
        member = (token >= start) & (token < end)
        turned = turned_ref[pl.ds(begin, WINDOW), :]
        turned = jnp.where(member, turned, jnp.zeros((), jnp.bfloat16))
        gradient = lax.dot_general(
            turned,
            projected_ref[pl.ds(begin, WINDOW), :],
            (((0,), (0,)), ((), ())),
            preferred_element_type=jnp.float32,
        )
        if sequence == 0:
            total_ref[...] = gradient * gradient
        elif sequence < SEQS - 1:
            total_ref[...] += gradient * gradient
        else:
            out_ref[...] = (total_ref[...] + gradient * gradient).reshape(out_ref.shape)


def gradients(starts, turned, projected, height):
    width = projected.shape[1]
    tile = 512
    out = pl.pallas_call(
        gradient_kernel,
        out_shape=jax.ShapeDtypeStruct((height, 1, width), jnp.float32),
        grid_spec=pltpu.PrefetchScalarGridSpec(
            num_scalar_prefetch=1,
            grid=(LANES // tile,),
            in_specs=[
                pl.BlockSpec((TOKENS, tile), lambda g, starts: (0, g)),
                pl.BlockSpec((TOKENS, width), lambda g, starts: (0, 0)),
            ],
            out_specs=pl.BlockSpec((tile, 1, width), lambda g, starts: (g, 0, 0)),
            scratch_shapes=[pltpu.VMEM((tile, width), jnp.float32)],
        ),
        compiler_params=pltpu.CompilerParams(vmem_limit_bytes=16 * 1024 * 1024),
    )(starts, turned, projected)
    return out.transpose(1, 0, 2)


def exchange(values, axis):
    return lax.all_to_all(values, axis, 0, 0, tiled=True)


def swap(values):
    return lax.ppermute(values, "core", [(i, CORES - 1 - i) for i in range(CORES)])


def body(hidden, unembed, rotate_vocab, rotate_width, labels, seq_ids):
    rows = unembed.shape[1]
    vocab, chip, core, width = (lax.axis_index(a).astype(jnp.int32) for a in ("vocab", "chip", "core", "width"))
    first = ((vocab * PARTS + chip * CORES) * rows).reshape(1)
    core = core.reshape(1)
    mine = lax.dynamic_slice_in_dim(labels, owned(core[0], width), BLOCK, 0).reshape(BLOCK, 1)
    sequence_index = jnp.arange(SEQS + 1, dtype=jnp.int32)
    starts = jnp.sum((seq_ids[None, :] < sequence_index[:, None]).astype(jnp.int32), axis=1)
    half, single = jnp.bfloat16, jnp.float32

    pieces = partial_sums(vocab.reshape(1), hidden, unembed, rotate_width)
    pieces = exchange(pieces, ("core", "width"))
    other = swap(rotate_vocab)
    logits, stats, share = call(
        functools.partial(local_kernel, rows),
        [((GROUP, LANES), single), ((1, 2, 128), single), ((CORES * SHARE, LANES), half)],
        [FULL, pl.BlockSpec(memory_space=pl.ANY)],
    )(pieces, other)
    stats = lax.all_gather(stats, "vocab", axis=0, tiled=True)
    stats = call(merge_kernel, [((1, 2, 128), single)], [FULL])(stats)
    stats = lax.all_gather(stats, "chip", axis=0, tiled=True)
    packed = call(
        functools.partial(error_kernel, rows),
        [((PARTS, CORES * ROWS, LANES), half)],
        [SCALARS, FULL, FULL, FULL, FULL],
    )(first, logits, stats, mine, share)
    turned, keep, send = call(
        turn_kernel,
        [((CHIPS, GROUP, LANES), half), ((PARTS * SHARE, LANES), half), ((PARTS * SHARE, LANES), half)],
        [SCALARS, FULL, FULL, FULL, pl.BlockSpec(memory_space=pl.ANY)],
    )(core, exchange(packed, "width"), rotate_vocab, other, starts)
    share = call(share_kernel, [((PARTS, GROUP, LANES), half)], [SCALARS, FULL, FULL])(core, keep, swap(send))
    projected = exchange(share, "vocab").reshape(TOKENS, LANES)
    turned = call(sum_kernel, [((GROUP, LANES), half)], [FULL])(exchange(turned, "chip"))
    turned = lax.all_gather(turned, ROW, axis=0, tiled=True)
    return gradients(starts, turned, projected, rows)


def solution(mesh):
    vocab, row, width = mesh.axis_names
    devices = mesh.devices.reshape(PARTS, CHIPS, CORES, PARTS)
    in_specs = (
        P(None, width),
        P(vocab, ROW, width),
        P(vocab, width, ROW),
        P(width, ROW),
        P(),
        P(),
    )
    return jax.shard_map(
        body,
        mesh=Mesh(devices, (vocab, *ROW, width)),
        in_specs=in_specs,
        out_specs=P(vocab, width, ROW),
        check_vma=False,
    )
```

```python
import functools

import jax
import jax.numpy as jnp
from jax import lax
from jax.experimental import pallas as pl
from jax.experimental.pallas import tpu as pltpu
from jax.sharding import Mesh
from jax.sharding import PartitionSpec as P

SEQ_LEN = 128
SEQS = 12
PARTS = 8
CORES = 2
CHIPS = PARTS // CORES
TOKENS = 768
GROUP = TOKENS // PARTS
BLOCK = GROUP // CORES
DEALT = BLOCK // PARTS
SHARE = 8
ROWS = BLOCK + SHARE
PAIRS = BLOCK // 2
LANES = 512
CHUNKS = 4
WINDOW = SEQ_LEN + 16
VMEM = 48 * 1024 * 1024
MOST = 60 * 1024 * 1024

FULL = pl.BlockSpec(memory_space=pltpu.VMEM)
SCALARS = pl.BlockSpec(memory_space=pltpu.SMEM)
ROW = ("chip", "core")


def call(kernel, outs, ins):
    shapes = [jax.ShapeDtypeStruct(s, d) for s, d in outs]
    return pl.pallas_call(
        kernel,
        out_shape=shapes if len(shapes) > 1 else shapes[0],
        in_specs=ins,
        out_specs=[FULL] * len(shapes) if len(shapes) > 1 else FULL,
        compiler_params=pltpu.CompilerParams(vmem_limit_bytes=VMEM),
    )


def pick(shape, source):
    row = lax.broadcasted_iota(jnp.int32, shape, 0)
    column = lax.broadcasted_iota(jnp.int32, shape, 1)
    return (column == source(row)).astype(jnp.float32).astype(jnp.bfloat16)


def owned(core, width):
    return (width // CORES * CORES + core) * GROUP + width % CORES * BLOCK


def step_of(exponent):
    return jnp.exp2(exponent)


def encode(values, bits):
    top, low = jnp.max(values, axis=1, keepdims=True), jnp.min(values, axis=1, keepdims=True)
    middle, radius = 0.5 * top + 0.5 * low, 0.5 * top - 0.5 * low
    least = jnp.maximum(radius / (0.97 * 2.0 ** (bits - 1)), jnp.abs(middle) * 2.0**-29)
    exponent = jnp.ceil(jnp.log2(jnp.maximum(least, 2.0**-100)))
    step = step_of(exponent)
    offset = jnp.floor(middle / step + 0.5)
    high = jnp.floor(offset / 32768.0)
    return jnp.floor((values - offset * step) / step + 0.5), (exponent, high, offset - high * 32768.0)


def whole(values):
    return values.astype(jnp.int32).astype(jnp.int16)


def partial_kernel(
    place_ref, hidden_hbm, unembed_hbm, width_hbm, out_ref, hidden_ref, unembed_ref, width_ref, logits_ref, sems
):
    rows = unembed_ref.shape[1]
    chunk = TOKENS // CHUNKS
    copies = [pltpu.make_async_copy(unembed_hbm, unembed_ref, sems.at[CHUNKS])]
    for number in range(CHUNKS):
        part = pl.ds(number * chunk, chunk)
        copies.append(pltpu.make_async_copy(hidden_hbm.at[part], hidden_ref.at[part], sems.at[number]))
    copies.append(pltpu.make_async_copy(width_hbm, width_ref, sems.at[CHUNKS + 1]))
    for copy in copies:
        copy.start()
    copies[0].wait()
    for number in range(CHUNKS):
        copies[1 + number].wait()
        part = slice(number * chunk, (number + 1) * chunk)
        logits_ref[part] = lax.dot_general(
            hidden_ref[part], unembed_ref[0], (((1,), (1,)), ((), ())), preferred_element_type=jnp.float32
        )
    copies[-1].wait()
    logits = logits_ref[...]
    mine = hidden_ref[pl.ds(pl.multiple_of(place_ref[0] * GROUP, GROUP), GROUP), :]

    def source(row):
        core, width, within = row // (PARTS * SHARE), lax.rem(row // SHARE, PARTS), lax.rem(row, SHARE)
        return jnp.where(within < DEALT, (width * CORES + core) * DEALT + within, -1)

    dealt = jnp.dot(pick((CORES * PARTS * SHARE, GROUP), source), mine, preferred_element_type=jnp.float32)
    projected = jnp.dot(dealt.astype(jnp.bfloat16), width_ref[...], preferred_element_type=jnp.float32)
    projected, share_notes = encode(projected, 16)
    logits, logit_notes = encode(logits, 24)
    high = jnp.floor(logits / 256.0 + 0.5)
    low = logits - high * 256.0
    lane = lax.broadcasted_iota(jnp.int32, (BLOCK, LANES - rows), 1)
    rest = jnp.zeros((BLOCK - SHARE, 1), jnp.float32)
    for core in range(CORES):
        for width in range(PARTS):
            owner, begin = core * PARTS + width, owned(core, width)
            tokens, shares = slice(begin, begin + BLOCK), slice(owner * SHARE, (owner + 1) * SHARE)
            notes = jnp.zeros((BLOCK, LANES - rows), jnp.float32)
            for number, part in enumerate(logit_notes):
                notes = jnp.where(lane == number, part[tokens], notes)
            for number, part in enumerate(share_notes):
                notes = jnp.where(lane == 3 + number, jnp.concatenate([part[shares], rest], axis=0), notes)
            out_ref[owner, :BLOCK, :rows] = whole(high[tokens])
            out_ref[owner, :BLOCK, rows:] = whole(notes)
            pairs = low[begin : begin + PAIRS] * 256.0 + (low[begin + PAIRS : begin + BLOCK] + 128.0)
            pairs = jnp.concatenate([pairs, jnp.zeros((PAIRS, LANES - rows), jnp.float32)], axis=1)
            out_ref[owner, BLOCK:, :] = whole(jnp.concatenate([pairs, projected[shares]], axis=0))


def partial_sums(place, hidden, unembed, rotate_width):
    anywhere = pl.BlockSpec(memory_space=pl.ANY)
    return pl.pallas_call(
        partial_kernel,
        out_shape=jax.ShapeDtypeStruct((CORES * PARTS, ROWS + PAIRS, LANES), jnp.int16),
        in_specs=[SCALARS, anywhere, anywhere, anywhere],
        out_specs=FULL,
        scratch_shapes=[
            pltpu.VMEM(hidden.shape, hidden.dtype),
            pltpu.VMEM(unembed.shape, unembed.dtype),
            pltpu.VMEM(rotate_width.shape, rotate_width.dtype),
            pltpu.VMEM((TOKENS, unembed.shape[1]), jnp.float32),
            pltpu.SemaphoreType.DMA((CHUNKS + 2,)),
        ],
        compiler_params=pltpu.CompilerParams(vmem_limit_bytes=MOST),
    )(place, hidden, unembed, rotate_width)


def decode(rows, pieces_ref, owner):
    high = pieces_ref[owner, :BLOCK].astype(jnp.int32).astype(jnp.float32)
    rest = pieces_ref[owner, BLOCK:].astype(jnp.int32).astype(jnp.float32)
    notes, pairs, share = high[:, rows:], rest[:PAIRS], rest[PAIRS:]
    first = jnp.floor(pairs / 256.0)
    low = jnp.concatenate([first, pairs - first * 256.0 - 128.0], axis=0)

    def offset(notes):
        return notes[:, 0:1] * 32768.0 + notes[:, 1:2]

    step = step_of(notes[:, 0:1])
    logits = (high * 256.0 + low) * step + offset(notes[:, 1:3]) * step
    step = step_of(notes[:SHARE, 3:4])
    share = share * step + offset(notes[:SHARE, 4:6]) * step
    return jnp.concatenate([logits, share], axis=0)


def local_kernel(rows, pieces_ref, unread_ref, logits_ref, stats_ref, share_ref):
    sums = [sum(decode(rows, pieces_ref, core * PARTS + width) for width in range(PARTS)) for core in range(CORES)]
    column = lax.broadcasted_iota(jnp.int32, (CORES * BLOCK, LANES), 1)
    logits = jnp.concatenate([part[:BLOCK] for part in sums], axis=0)
    logits = jnp.where(column < rows, logits, -jnp.inf)
    logits_ref[...] = logits
    share_ref[...] = jnp.concatenate([part[BLOCK:] for part in sums], axis=0).astype(jnp.bfloat16)
    largest = jnp.max(logits, axis=1, keepdims=True)
    largest = jnp.maximum(largest[:BLOCK], largest[BLOCK:])
    total = jnp.sum(jnp.exp(logits - jnp.concatenate([largest, largest], axis=0)), axis=1, keepdims=True)
    total = total[:BLOCK] + total[BLOCK:]
    lane = lax.broadcasted_iota(jnp.int32, (BLOCK, 128), 1)
    square = jnp.concatenate(
        [jnp.where(lane == 0, largest, total), jnp.zeros((128 - BLOCK, 128), jnp.float32)], axis=0
    )
    tile = square.T[: stats_ref.shape[1]]
    for device in range(stats_ref.shape[0]):
        stats_ref[device] = tile


def merge_kernel(stats_ref, out_ref):
    largest = jnp.max(stats_ref[:, 0:1, :], axis=0)
    total = jnp.sum(stats_ref[:, 1:2, :] * jnp.exp(stats_ref[:, 0:1, :] - largest[None]), axis=0)
    out_ref[0] = jnp.concatenate([largest, total], axis=0)


def error_kernel(rows, first_ref, logits_ref, stats_ref, labels_ref, share_ref, out_ref):
    largest = jnp.max(stats_ref[:, 0:1, :], axis=0)
    total = jnp.sum(stats_ref[:, 1:2, :] * jnp.exp(stats_ref[:, 0:1, :] - largest[None]), axis=0)
    row = lax.broadcasted_iota(jnp.int32, (128, 128), 0)
    square = jnp.where(row == 0, largest, total).T
    largest, total = square[:BLOCK, 0:1], square[:BLOCK, 1:2]
    column = lax.broadcasted_iota(jnp.int32, (BLOCK, LANES), 1)
    parts = []
    for core in range(CORES):
        probabilities = jnp.exp(logits_ref[core * BLOCK : (core + 1) * BLOCK] - largest) / total
        hit = (labels_ref[...] - (first_ref[0] + core * rows) == column) & (column < rows)
        parts.append((probabilities - hit.astype(jnp.float32)).astype(jnp.bfloat16))
    errors = jnp.concatenate(parts, axis=0)
    for piece in range(PARTS):
        out_ref[piece, : CORES * BLOCK] = errors
        out_ref[piece, CORES * BLOCK :] = share_ref[...]


def turn_kernel(core_ref, packed_ref, basis_ref, other_ref, starts_ref, out_ref, keep_ref, send_ref):
    rows = basis_ref.shape[1]
    turned = 0.0
    for core, ref in ((core_ref[0], basis_ref), (1 - core_ref[0], other_ref)):
        errors = packed_ref[:, pl.ds(pl.multiple_of(core * BLOCK, BLOCK), BLOCK), :].reshape(PARTS * BLOCK, LANES)
        turned += lax.dot_general(
            errors[:, :rows], ref[0], (((1,), (1,)), ((), ())), preferred_element_type=jnp.float32
        )
    out_ref[:, :, :rows] = turned.astype(jnp.bfloat16).reshape(CHIPS, GROUP, rows)
    out_ref[:, :, rows:] = jnp.zeros((CHIPS, GROUP, LANES - rows), jnp.bfloat16)
    share = packed_ref[:, GROUP:, :].astype(jnp.float32)
    first, second = share[:, :SHARE], share[:, SHARE:]
    first_core = core_ref[0] == 0
    keep, send = jnp.where(first_core, first, second), jnp.where(first_core, second, first)
    keep_ref[...] = keep.reshape(PARTS * SHARE, LANES).astype(jnp.bfloat16)
    send_ref[...] = send.reshape(PARTS * SHARE, LANES).astype(jnp.bfloat16)


def share_kernel(core_ref, keep_ref, got_ref, out_ref):
    def order(core):
        def source(row):
            owner, within = row // DEALT, lax.rem(row, DEALT)
            return jnp.where(lax.rem(owner, CORES) == core, owner // CORES * SHARE + within, -1)

        return pick((GROUP, PARTS * SHARE), source)

    core = core_ref[0]
    share = jnp.dot(order(core), keep_ref[...], preferred_element_type=jnp.float32)
    share += jnp.dot(order(1 - core), got_ref[...], preferred_element_type=jnp.float32)
    share = share.astype(jnp.bfloat16)
    for piece in range(PARTS):
        out_ref[piece] = share


def sum_kernel(pieces_ref, out_ref):
    out_ref[...] = jnp.sum(pieces_ref[...].astype(jnp.float32), axis=0).astype(jnp.bfloat16)


def gradient_kernel(starts_ref, turned_ref, projected_ref, out_ref, total_ref):
    for sequence in range(SEQS):
        start, end = starts_ref[sequence], starts_ref[sequence + 1]
        begin = pl.multiple_of(jnp.minimum(start // 16 * 16, TOKENS - WINDOW), 16)
        token = begin + lax.broadcasted_iota(jnp.int32, (WINDOW, 1), 0)
        member = (token >= start) & (token < end)
        turned = turned_ref[pl.ds(begin, WINDOW), :]
        turned = jnp.where(member, turned, jnp.zeros((), jnp.bfloat16))
        gradient = lax.dot_general(
            turned,
            projected_ref[pl.ds(begin, WINDOW), :],
            (((0,), (0,)), ((), ())),
            preferred_element_type=jnp.float32,
        )
        if sequence == 0:
            total_ref[...] = gradient * gradient
        elif sequence < SEQS - 1:
            total_ref[...] += gradient * gradient
        else:
            out_ref[...] = (total_ref[...] + gradient * gradient).reshape(out_ref.shape)


def gradients(starts, turned, projected, height):
    width = projected.shape[1]
    tile = 512
    out = pl.pallas_call(
        gradient_kernel,
        out_shape=jax.ShapeDtypeStruct((height, 1, width), jnp.float32),
        grid_spec=pltpu.PrefetchScalarGridSpec(
            num_scalar_prefetch=1,
            grid=(LANES // tile,),
            in_specs=[
                pl.BlockSpec((TOKENS, tile), lambda g, starts: (0, g)),
                pl.BlockSpec((TOKENS, width), lambda g, starts: (0, 0)),
            ],
            out_specs=pl.BlockSpec((tile, 1, width), lambda g, starts: (g, 0, 0)),
            scratch_shapes=[pltpu.VMEM((tile, width), jnp.float32)],
        ),
        compiler_params=pltpu.CompilerParams(vmem_limit_bytes=16 * 1024 * 1024),
    )(starts, turned, projected)
    return out.transpose(1, 0, 2)


def exchange(values, axis):
    return lax.all_to_all(values, axis, 0, 0, tiled=True)


def swap(values):
    return lax.ppermute(values, "core", [(i, CORES - 1 - i) for i in range(CORES)])


def body(hidden, unembed, rotate_vocab, rotate_width, labels, seq_ids):
    rows = unembed.shape[1]
    vocab, chip, core, width = (lax.axis_index(a).astype(jnp.int32) for a in ("vocab", "chip", "core", "width"))
    first = ((vocab * PARTS + chip * CORES) * rows).reshape(1)
    core = core.reshape(1)
    mine = lax.dynamic_slice_in_dim(labels, owned(core[0], width), BLOCK, 0).reshape(BLOCK, 1)
    sequence_index = jnp.arange(SEQS + 1, dtype=jnp.int32)
    starts = jnp.sum((seq_ids[None, :] < sequence_index[:, None]).astype(jnp.int32), axis=1)
    half, single = jnp.bfloat16, jnp.float32

    pieces = partial_sums(vocab.reshape(1), hidden, unembed, rotate_width)
    pieces = exchange(pieces, ("core", "width"))
    other = swap(rotate_vocab)
    logits, stats, share = call(
        functools.partial(local_kernel, rows),
        [((GROUP, LANES), single), ((1, 2, 128), single), ((CORES * SHARE, LANES), half)],
        [FULL, pl.BlockSpec(memory_space=pl.ANY)],
    )(pieces, other)
    stats = lax.all_gather(stats, "vocab", axis=0, tiled=True)
    stats = call(merge_kernel, [((1, 2, 128), single)], [FULL])(stats)
    stats = lax.all_gather(stats, "chip", axis=0, tiled=True)
    packed = call(
        functools.partial(error_kernel, rows),
        [((PARTS, CORES * ROWS, LANES), half)],
        [SCALARS, FULL, FULL, FULL, FULL],
    )(first, logits, stats, mine, share)
    turned, keep, send = call(
        turn_kernel,
        [((CHIPS, GROUP, LANES), half), ((PARTS * SHARE, LANES), half), ((PARTS * SHARE, LANES), half)],
        [SCALARS, FULL, FULL, FULL, pl.BlockSpec(memory_space=pl.ANY)],
    )(core, exchange(packed, "width"), rotate_vocab, other, starts)
    share = call(share_kernel, [((PARTS, GROUP, LANES), half)], [SCALARS, FULL, FULL])(core, keep, swap(send))
    projected = exchange(share, "vocab").reshape(TOKENS, LANES)
    turned = call(sum_kernel, [((GROUP, LANES), half)], [FULL])(exchange(turned, "chip"))
    turned = lax.all_gather(turned, ROW, axis=0, tiled=True)
    return gradients(starts, turned, projected, rows)


def solution(mesh):
    vocab, row, width = mesh.axis_names
    devices = mesh.devices.reshape(PARTS, CHIPS, CORES, PARTS)
    in_specs = (
        P(None, width),
        P(vocab, ROW, width),
        P(vocab, width, ROW),
        P(width, ROW),
        P(),
        P(),
    )
    return jax.shard_map(
        body,
        mesh=Mesh(devices, (vocab, *ROW, width)),
        in_specs=in_specs,
        out_specs=P(vocab, width, ROW),
        check_vma=False,
    )
```
